32 devices in a mesh: rep: 8 (over y, x, core), shard: 4 (over z).
Axes of the slice: x: 2, y: 2, z: 4, core: 2. Of those that a mesh axis runs over, the one named last changes fastest.
Arguments:
- tokens: bfloat16 [8192, 2048], P(('rep', 'shard')), may hold values from -6 to 6
- cotangent: bfloat16 [8192, 2048], P(('rep', 'shard')), may hold values from -6 to 6
- segments: int32 [32, 256], P(('rep', 'shard')), may hold values from 0 to 3, never falling along the last dimension, each value on 1 to 128 neighbouring positions
- padding: int32 [32, 256], P(('rep', 'shard')), may hold values from 0 to 1, as said below
- routes: int32 [8192, 8], P(('rep', 'shard')), may hold values from 0 to 15, all different within a row; in each aligned block of 256 rows (0 to 255, 256 to 511, ...) at most 160 rows name the same one
- route_weights: float32 [8192, 8], P(('rep', 'shard')), may hold values from 0.05 to 0.3
- adapter_set: int32 [32], P(('rep', 'shard')), may hold values from 0 to 1
- norm_one: float32 [2048], replicated, may hold values from 0.1 to 1.9
- norm_two: float32 [2048], replicated, may hold values from 0.1 to 1.9
- query_weight: bfloat16 [2048, 2048], P(None, 'shard'), may hold values from -0.125 to 0.125
- key_weight: bfloat16 [2048, 2048], P(None, 'shard'), may hold values from -0.125 to 0.125
- value_weight: bfloat16 [2048, 2048], P(None, 'shard'), may hold values from -0.125 to 0.125
- output_weight: bfloat16 [2048, 2048], P(None, 'shard'), may hold values from -0.5 to 0.5
- query_down: bfloat16 [2048, 2, 16], P('shard'), may hold values from -0.125 to 0.125
- key_down: bfloat16 [2048, 2, 16], P('shard'), may hold values from -0.125 to 0.125
- value_down: bfloat16 [2048, 2, 16], P('shard'), may hold values from -0.125 to 0.125
- output_down: bfloat16 [2048, 2, 16], P('shard'), may hold values from -0.125 to 0.125
- query_lift: bfloat16 [2048, 2, 16], P('shard'), may hold values from -0.75 to 0.75
- key_lift: bfloat16 [2048, 2, 16], P('shard'), may hold values from -0.75 to 0.75
- value_lift: bfloat16 [2048, 2, 16], P('shard'), may hold values from -0.75 to 0.75
- output_lift: bfloat16 [2048, 2, 16], P('shard'), may hold values from -1.5 to 1.5
- expert_gate: bfloat16 [16, 2048, 1024], P('shard'), may hold values from -0.125 to 0.125
- expert_upper: bfloat16 [16, 2048, 1024], P('shard'), may hold values from -0.125 to 0.125
- expert_lower: bfloat16 [16, 1024, 2048], P('shard'), may hold values from -0.1875 to 0.1875
- gate_down: bfloat16 [16, 2048, 2, 16], P('shard'), may hold values from -0.125 to 0.125
- gate_lift: bfloat16 [16, 1024, 2, 16], P('shard'), may hold values from -0.75 to 0.75
- upper_down: bfloat16 [16, 2048, 2, 16], P('shard'), may hold values from -0.125 to 0.125
- upper_lift: bfloat16 [16, 1024, 2, 16], P('shard'), may hold values from -0.75 to 0.75
- lower_down: bfloat16 [16, 1024, 2, 16], P('shard'), may hold values from -0.1875 to 0.1875
- lower_lift: bfloat16 [16, 2048, 2, 16], P('shard'), may hold values from -0.75 to 0.75
Outputs:
- output: bfloat16 [8192, 2048], P(('rep', 'shard'))
- input_grad: bfloat16 [8192, 2048], P(('rep', 'shard'))
- query_down_grad: float32 [2048, 2, 16], P('shard')
- key_down_grad: float32 [2048, 2, 16], P('shard')
- value_down_grad: float32 [2048, 2, 16], P('shard')
- output_down_grad: float32 [2048, 2, 16], P('shard')
- query_lift_grad: float32 [2048, 2, 16], P('shard')
- key_lift_grad: float32 [2048, 2, 16], P('shard')
- value_lift_grad: float32 [2048, 2, 16], P('shard')
- output_lift_grad: float32 [2048, 2, 16], P('shard')
- gate_down_grad: float32 [16, 2048, 2, 16], P('shard')
- gate_lift_grad: float32 [16, 1024, 2, 16], P('shard')
- upper_down_grad: float32 [16, 2048, 2, 16], P('shard')
- upper_lift_grad: float32 [16, 1024, 2, 16], P('shard')
- lower_down_grad: float32 [16, 1024, 2, 16], P('shard')
- lower_lift_grad: float32 [16, 2048, 2, 16], P('shard')
The draws below stay inside these ranges and needn't reach their ends.
Inputs may be any that keep to these rules, and one draw needn't show every extreme that they name: `routes`: in the 256 rows of one sequence no expert is named by more than 160 rows, a bound that some block reaches; a row's 8 experts differ. `segments`: within a sequence the entries never fall. `padding`: each row of 256 is 1 up to some position and 0 after it, with at most 64 zeros.
All inputs are finite; a program needn't handle non-finite values.
Results may differ from the reference program's by a relative error of at most 0.023.
Values may be sent and summed in bfloat16 or wider, within the bound.
No kernel may reach another device: no remote copies, remote signals or barrier semaphores. Data moves between devices by JAX's collectives and lax.ppermute only.
A program may use at most 384 MiB of HBM per device.

```python
import math
import jax
import jax.numpy as jnp
import numpy as np
from jax import lax

D = 2048
HEADS = 16
HEAD = 128
FF = 1024
TOP = 8
EXPERTS = 16
RANK = 16
SETS = 2
TOK_DEV = 256
MOST = 160
SEQS = 32
TOKENS = 8192


def draw_padding(key, part):
    cut_count = jax.random.randint(key, (SEQS, 1), 0, TOK_DEV // 4 + 1)
    positions = jnp.arange(TOK_DEV, dtype=jnp.int32)[None, :]
    return (positions < TOK_DEV - cut_count).astype(jnp.int32)


def set_ends(entries, key, least, high):
    longest = entries.shape.index(max(entries.shape))
    spots = []
    for shift in (0, 1):
        where = [jax.random.randint(jax.random.fold_in(key, axis), (), 0, length) for axis, length in enumerate(entries.shape)]
        where[longest] = (where[longest] + shift) % entries.shape[longest]
        spots.append(tuple(where))
    return entries.at[spots[0]].set(least).at[spots[1]].set(high)


def block_scale(key, extent, cuts, smallest, top_value):
    def one(position, parts):
        draws = jax.random.uniform(jax.random.fold_in(jax.random.fold_in(key, 6), position), (parts,), jnp.float32, smallest / len(cuts), top_value / len(cuts))
        return jnp.repeat(jnp.exp(draws), extent[position] // parts).reshape((-1,) + (1,) * (len(extent) - position - 1))

    loudness = one(*cuts[0])
    for cut in cuts[1:]:
        loudness = loudness * one(*cut)
    return loudness


def profile(number_of, total, most, slope):
    loads = [(1 << 20) // math.isqrt(standing ** slope) + 1 for standing in range(2, number_of + 1)]
    spare, given = total - most - (number_of - 1), [1] * (number_of - 1)
    while spare > 0:
        free = [i for i in range(number_of - 1) if given[i] < most]
        mass, left = sum([loads[i] for i in free]), spare
        for i in free:
            extra = min(most - given[i], max(1, left * loads[i] // mass), spare)
            given[i] = given[i] + extra
            spare = spare - extra
    return np.array([most] + given)


def ragged_sizes(own_key, count, total, bound, lean):
    if count == 2:
        one = jax.random.randint(own_key, (), max(1, total - bound), min(bound, total - 1) + 1)
        return jnp.stack([one, total - one])
    lengths = jnp.asarray(profile(count, total, bound, lean), jnp.int32)
    pairs = (count - 1) // 2
    donor, sink = lengths[1:1 + 2 * pairs:2], lengths[2:2 + 2 * pairs:2]
    slack = jnp.minimum(donor - 1, bound - sink)
    moved = jax.random.randint(jax.random.fold_in(own_key, 1), (pairs,), 0, 1 << 20) % (slack + 1)
    lengths = lengths.at[1:1 + 2 * pairs:2].set(donor - moved).at[2:2 + 2 * pairs:2].set(sink + moved)
    return lengths[jax.random.permutation(jax.random.fold_in(own_key, 2), count)]


def assign_block(stream_key, own, number, rows, number_of, top, reach, skew):
    order = jax.random.permutation(stream_key, number_of)
    crowded, ordinary = load_shares(number_of, rows * top, reach, skew, True), load_shares(number_of, rows * top, reach, skew, False)
    places = jnp.arange(number_of)

    def named(lengths, turn):
        used = int((lengths > 0).sum())
        fixed = max(1, used // 4)
        passed = fixed + (places - fixed + turn * (used - fixed)) % max(1, number_of - fixed)
        return jnp.zeros((number_of,), jnp.int32).at[order[jnp.where(places < fixed, places, passed)]].set(jnp.asarray(lengths, jnp.int32))

    lengths = jnp.where(number % 4 == 0, named(crowded, number // 4), named(ordinary, number - number // 4 - 1))
    mixed = jax.random.permutation(jax.random.fold_in(own, 3), number_of)
    donor, taker = mixed[0:number_of // 2 * 2:2], mixed[1:number_of // 2 * 2:2]
    margin = jnp.minimum(lengths[donor] - 1, reach - lengths[taker]) // 2
    margin = jnp.where((donor == order[0]) | (taker == order[0]) | (lengths[taker] == 0), 0, jnp.maximum(margin, 0))
    passed = jax.random.randint(jax.random.fold_in(own, 4), (number_of // 2,), 0, 1 << 20) % (margin + 1)
    lengths = lengths.at[donor].add(-passed).at[taker].add(passed)
    labels = jnp.searchsorted(jnp.cumsum(lengths), jnp.arange(rows * top), side="right").astype(jnp.int32)
    table = labels.reshape(top, rows).T
    table = table[jax.random.permutation(jax.random.fold_in(own, 1), rows)]
    turn = jax.random.randint(jax.random.fold_in(own, 2), (rows, 1), 0, top)
    return jnp.take_along_axis(table, (jnp.arange(top)[None, :] + turn) % top, axis=1)


def load_shares(count, total, bound, skew, full):
    portions = [(1 << 20) // math.isqrt(standing ** skew) + 1 for standing in range(1, count + 1)]
    largest = bound if full else min(bound, max(-(-total // count), total * portions[0] // sum(portions)))
    least = 1 if total - largest >= count - 1 else 0
    holding, surplus = [largest] + [least] * (count - 1), total - largest - least * (count - 1)
    while surplus > 0:
        free = [i for i in range(1, count) if holding[i] < largest] or [i for i in range(1, count) if holding[i] < bound]
        mass, left = sum([portions[i] for i in free]), surplus
        for i in free:
            more = min(bound - holding[i], max(1, left * portions[i] // mass), surplus)
            holding[i] = holding[i] + more
            surplus = surplus - more
    return np.array(holding)


def bell_draw(own_key, extent, scale, limit, cuts=(), held_as=jnp.bfloat16):
    loudness = block_scale(own_key, extent, cuts, -0.22, 0.18) if cuts else 1.0
    array = jax.random.normal(own_key, extent, jnp.float32) * scale * loudness
    return jnp.minimum(jnp.maximum(array, -limit), limit).astype(held_as)


def setup_inputs(seed: int = 0) -> dict:
    splits = jax.random.split(jax.random.key(seed), 31)
    tokens = bell_draw(splits[0], (TOKENS, D), 1.0, 6.0, ((0, 32),))
    cotangent = bell_draw(splits[1], (TOKENS, D), 1.0, 6.0, ((0, 32),))
    segments = jax.vmap(lambda own: jnp.searchsorted(jnp.cumsum(ragged_sizes(own, 4, TOK_DEV, TOK_DEV // 2, 2)), jnp.arange(TOK_DEV), side="right"))(jax.random.split(splits[2], SEQS)).reshape((SEQS, TOK_DEV)).astype(jnp.int32)
    padding = draw_padding(jax.random.fold_in(splits[30], 71), 0)
    routes_keys = jax.random.split(jax.random.fold_in(splits[4], 1), TOKENS // TOK_DEV)
    routes_turns = jax.random.permutation(jax.random.fold_in(splits[4], 3), TOKENS // TOK_DEV)
    routes = jax.vmap(lambda own, number: assign_block(jax.random.fold_in(splits[4], 2), own, number, TOK_DEV, EXPERTS, TOP, MOST, 1))(routes_keys, routes_turns).reshape((TOKENS, TOP))
    route_weights = jnp.clip(0.05 + 0.25 * jax.random.uniform(splits[5], (TOKENS, TOP), jnp.float32) ** block_scale(splits[5], (TOKENS, TOP), ((0, 32),), -0.2, 0.2), 0.05, 0.3)
    adapter_set = set_ends(jax.random.randint(splits[6], (SEQS,), 0, SETS), jax.random.fold_in(splits[6], 1), 0, SETS - 1).astype(jnp.int32)
    norm_one = jnp.clip(1.0 + 0.18 * jax.random.normal(splits[7], (D,), jnp.float32), 0.1, 1.9)
    norm_two = jnp.clip(1.0 + 0.18 * jax.random.normal(splits[8], (D,), jnp.float32), 0.1, 1.9)
    query_weight = bell_draw(splits[9], (D, D), D ** -0.5, 0.125, ((1, 4),))
    key_weight = bell_draw(splits[10], (D, D), D ** -0.5, 0.125, ((1, 4),))
    value_weight = bell_draw(splits[11], (D, D), D ** -0.5, 0.125, ((1, 4),))
    output_weight = bell_draw(splits[12], (D, D), (D // 16) ** -0.5, 0.5, ((1, 4),))
    query_down = bell_draw(splits[13], (D, SETS, RANK), D ** -0.5, 0.125, ((0, 4),))
    key_down = bell_draw(splits[14], (D, SETS, RANK), D ** -0.5, 0.125, ((0, 4),))
    value_down = bell_draw(splits[15], (D, SETS, RANK), D ** -0.5, 0.125, ((0, 4),))
    output_down = bell_draw(splits[16], (D, SETS, RANK), D ** -0.5, 0.125, ((0, 4),))
    query_lift = bell_draw(splits[17], (D, SETS, RANK), (4 * RANK) ** -0.5, 0.75, ((0, 4),))
    key_lift = bell_draw(splits[18], (D, SETS, RANK), (4 * RANK) ** -0.5, 0.75, ((0, 4),))
    value_lift = bell_draw(splits[19], (D, SETS, RANK), (4 * RANK) ** -0.5, 0.75, ((0, 4),))
    output_lift = bell_draw(splits[20], (D, SETS, RANK), RANK ** -0.5, 1.5, ((0, 4),))
    expert_gate = bell_draw(splits[21], (EXPERTS, D, FF), D ** -0.5, 0.125, ((0, 4),))
    expert_upper = bell_draw(splits[22], (EXPERTS, D, FF), D ** -0.5, 0.125, ((0, 4),))
    expert_lower = bell_draw(splits[23], (EXPERTS, FF, D), FF ** -0.5, 0.1875, ((0, 4),))
    gate_down = bell_draw(splits[24], (EXPERTS, D, SETS, RANK), D ** -0.5, 0.125, ((0, 4),))
    gate_lift = bell_draw(splits[25], (EXPERTS, FF, SETS, RANK), (4 * RANK) ** -0.5, 0.75, ((0, 4),))
    upper_down = bell_draw(splits[26], (EXPERTS, D, SETS, RANK), D ** -0.5, 0.125, ((0, 4),))
    upper_lift = bell_draw(splits[27], (EXPERTS, FF, SETS, RANK), (4 * RANK) ** -0.5, 0.75, ((0, 4),))
    lower_down = bell_draw(splits[28], (EXPERTS, FF, SETS, RANK), FF ** -0.5, 0.1875, ((0, 4),))
    lower_lift = bell_draw(splits[29], (EXPERTS, D, SETS, RANK), (4 * RANK) ** -0.5, 0.75, ((0, 4),))
    return {"tokens": tokens, "cotangent": cotangent, "segments": segments, "padding": padding, "routes": routes, "route_weights": route_weights, "adapter_set": adapter_set, "norm_one": norm_one, "norm_two": norm_two, "query_weight": query_weight, "key_weight": key_weight, "value_weight": value_weight, "output_weight": output_weight, "query_down": query_down, "key_down": key_down, "value_down": value_down, "output_down": output_down, "query_lift": query_lift, "key_lift": key_lift, "value_lift": value_lift, "output_lift": output_lift, "expert_gate": expert_gate, "expert_upper": expert_upper, "expert_lower": expert_lower, "gate_down": gate_down, "gate_lift": gate_lift, "upper_down": upper_down, "upper_lift": upper_lift, "lower_down": lower_down, "lower_lift": lower_lift}


@jax.custom_vjp
def low(v):
    return lax.optimization_barrier(v.astype(jnp.bfloat16)).astype(jnp.float32)

@jax.custom_vjp
def low_back(v):
    return v

def low_keep(v):
    return (low(v), None)

def low_pass(kept, grad):
    return (grad,)

def back_keep(v):
    return (v, None)

def back_low(kept, grad):
    return (low(grad),)
low.defvjp(low_keep, low_pass)
low_back.defvjp(back_keep, back_low)
epsilon = 1e-06
adapter_scale = 2.0
masked_score = -1e+30

def both_ways(values):
    return low(low_back(values))

def precise_product(left, right):
    return jnp.dot(left, right, precision=lax.Precision.HIGHEST, preferred_element_type=jnp.float32)

def rms_norm(values, gain_vec):
    return values * lax.rsqrt(lax.optimization_barrier(jnp.mean(values * values, axis=-1, keepdims=True)) + epsilon) * gain_vec

def adapt_plain(block_of_rows, dense_weight, down, raise_matrix):
    narrowed_rows = both_ways(precise_product(block_of_rows, down))
    return precise_product(block_of_rows, dense_weight) + adapter_scale * precise_product(narrowed_rows, raise_matrix.T)

def adapt_batch(block_of_rows, dense_weight, down, raise_matrix):
    highest_precision = lax.Precision.HIGHEST
    narrowed_rows = both_ways(jnp.einsum('eci,eir->ecr', block_of_rows, down, precision=highest_precision))
    frozen_output = jnp.einsum('eci,eio->eco', block_of_rows, dense_weight, precision=highest_precision)
    return frozen_output + adapter_scale * jnp.einsum('hzq,hkq->hzk', narrowed_rows, raise_matrix, precision=highest_precision)

def route_slots(routes, route_weights):
    expert_ids = jnp.arange(EXPERTS, dtype=jnp.int32)
    picked = (routes[:, :, None] == expert_ids[None, None, :]).astype(jnp.int32)
    member = lax.optimization_barrier(jnp.sum(picked, axis=1))
    before = jnp.cumsum(member, axis=0) - member
    slot_of = lax.optimization_barrier(jnp.sum(picked * (expert_ids[None, None, :] * MOST + before[:, None, :]), axis=2))
    slot_ids = jnp.arange(MOST, dtype=jnp.int32)
    chosen = member.T[:, None, :] * (before.T[:, None, :] == slot_ids[None, :, None]).astype(jnp.int32)
    token_ids = jnp.arange(routes.shape[0], dtype=jnp.int32)
    token_of = lax.optimization_barrier(jnp.sum(chosen * token_ids[None, None, :], axis=2))
    return (slot_of, token_of)

def one_sequence(frozen, trained, data):
    norm_one, norm_two, query_weight, key_weight, value_weight, output_weight, expert_gate, expert_upper, expert_lower = frozen
    query_down, key_down, value_down, output_down, query_lift, key_lift, value_lift, output_lift, gate_down, gate_lift, upper_down, upper_lift, lower_down, lower_lift = trained
    residual, segment_ids, real_keys, routes, route_weights, chosen_set = data
    seq_len = residual.shape[0]
    highest_precision = lax.Precision.HIGHEST

    def pick(table):
        return lax.dynamic_index_in_dim(table, chosen_set, 1, keepdims=False)

    def pick_expert(table):
        return lax.dynamic_index_in_dim(table, chosen_set, 2, keepdims=False)
    normed_one = low(rms_norm(residual, norm_one))
    heads_q = both_ways(adapt_plain(normed_one, query_weight, pick(query_down), pick(query_lift))).reshape(seq_len, HEADS, HEAD)
    heads_k = both_ways(adapt_plain(normed_one, key_weight, pick(key_down), pick(key_lift))).reshape(seq_len, HEADS, HEAD)
    heads_v = both_ways(adapt_plain(normed_one, value_weight, pick(value_down), pick(value_lift))).reshape(seq_len, HEADS, HEAD)
    logits = low_back(jnp.einsum('qhd,khd->hqk', heads_q, heads_k, precision=highest_precision) * HEAD ** (-0.5))
    positions = jnp.arange(seq_len, dtype=jnp.int32)
    allowed = (segment_ids[:, None] == segment_ids[None, :]) & ((real_keys[None, :] == 1) | (positions[:, None] == positions[None, :]))
    logits = jnp.where(allowed[None], logits, masked_score)
    attn_probs = low(jax.nn.softmax(logits, axis=-1))
    attn_mixed = both_ways(jnp.einsum('hqk,khd->qhd', attn_probs, heads_v, precision=highest_precision).reshape(seq_len, HEADS * HEAD))
    after_attn = residual + low_back(adapt_plain(attn_mixed, output_weight, pick(output_down), pick(output_lift)))
    normed_two = low(rms_norm(after_attn, norm_two))
    slot_of, token_of = route_slots(routes, route_weights)
    dispatched = low_back(jnp.take(normed_two, token_of.reshape(-1), axis=0).reshape(EXPERTS, MOST, -1))
    gate_val = low_back(adapt_batch(dispatched, expert_gate, pick_expert(gate_down), pick_expert(gate_lift)))
    upper_val = low_back(adapt_batch(dispatched, expert_upper, pick_expert(upper_down), pick_expert(upper_lift)))
    hidden = low(jax.nn.silu(gate_val) * upper_val)
    expert_out = both_ways(adapt_batch(hidden, expert_lower, pick_expert(lower_down), pick_expert(lower_lift)))
    picked_rows = jnp.take(expert_out.reshape(EXPERTS * MOST, -1), slot_of.reshape(-1), axis=0).reshape(seq_len, TOP, -1)
    return after_attn + lax.optimization_barrier(jnp.sum(picked_rows * route_weights[:, :, None], axis=1))

def to_float(values):
    return values.astype(jnp.float32)

def reference(tokens, cotangent, segments, padding, routes, route_weights, adapter_set, norm_one, norm_two, query_weight, key_weight, value_weight, output_weight, query_down, key_down, value_down, output_down, query_lift, key_lift, value_lift, output_lift, expert_gate, expert_upper, expert_lower, gate_down, gate_lift, upper_down, upper_lift, lower_down, lower_lift):
    frozen = (to_float(norm_one), to_float(norm_two), to_float(query_weight), to_float(key_weight), to_float(value_weight), to_float(output_weight), to_float(expert_gate), to_float(expert_upper), to_float(expert_lower))
    trained = (to_float(query_down), to_float(key_down), to_float(value_down), to_float(output_down), to_float(query_lift), to_float(key_lift), to_float(value_lift), to_float(output_lift), to_float(gate_down), to_float(gate_lift), to_float(upper_down), to_float(upper_lift), to_float(lower_down), to_float(lower_lift))
    seq_count = adapter_set.shape[0]
    token_blocks = to_float(tokens).reshape(seq_count, -1, D)
    rest = (segments, padding, routes.reshape(seq_count, -1, TOP), to_float(route_weights).reshape(seq_count, -1, TOP), adapter_set)

    def forward(token_all, trained_all):

        def stepper(item_data):
            return one_sequence(frozen, trained_all, item_data)
        return lax.map(jax.checkpoint(stepper), (token_all,) + rest)
    outputs, pullback = jax.vjp(forward, token_blocks, trained)
    grad_tokens, grad_trained = pullback(to_float(cotangent).reshape(seq_count, -1, D))
    return (outputs.reshape(-1, D).astype(jnp.bfloat16), grad_tokens.reshape(-1, D).astype(jnp.bfloat16), grad_trained[0], grad_trained[1], grad_trained[2], grad_trained[3], grad_trained[4], grad_trained[5], grad_trained[6], grad_trained[7], grad_trained[8], grad_trained[9], grad_trained[10], grad_trained[11], grad_trained[12], grad_trained[13])
```

```python
import functools

import jax
import jax.numpy as jnp
from jax import lax
from jax.experimental import pallas as pl
from jax.experimental.pallas import tpu as pltpu
from jax.sharding import PartitionSpec as P

HEADS = 16
HEAD = 128
TOP = 8
EXPERTS = 16
RANK = 16
SETS = 2
MOST = 160
PACK = SETS * RANK

epsilon = 1e-06
adapter_scale = 2.0
masked_score = -1e30
score_scale = HEAD ** (-0.5)

BF = jnp.bfloat16
F32 = jnp.float32
VMEM = 56 * 1024 * 1024


def dot_nn(a, b):
    return jnp.dot(a, b, preferred_element_type=F32)


def dot_nt(a, b):
    return lax.dot_general(a, b, (((1,), (1,)), ((), ())), preferred_element_type=F32)


def dot_tn(a, b):
    return lax.dot_general(a, b, (((0,), (0,)), ((), ())), preferred_element_type=F32)


def rms_forward(values, gain_vec):
    inverse = lax.rsqrt(jnp.mean(values * values, axis=-1, keepdims=True) + epsilon)
    return values * inverse * gain_vec


def rms_backward(values, gain_vec, grad_norm):
    inverse = lax.rsqrt(jnp.mean(values * values, axis=-1, keepdims=True) + epsilon)
    weighted = grad_norm * gain_vec
    cubed = inverse * inverse * inverse
    return inverse * weighted - values * cubed * jnp.mean(values * weighted, axis=-1, keepdims=True)


def scores(q, k, allowed):
    s = dot_nt(q, k) * score_scale
    s = jnp.where(allowed, s, masked_score)
    e = jnp.exp(s - jnp.max(s, axis=-1, keepdims=True))
    return e / jnp.sum(e, axis=-1, keepdims=True)


def allowed_mask(seg_row, seg_col, pad_row):
    rows = lax.broadcasted_iota(jnp.int32, (seg_col.shape[0], seg_row.shape[1]), 0)
    cols = lax.broadcasted_iota(jnp.int32, (seg_col.shape[0], seg_row.shape[1]), 1)
    return (seg_col == seg_row) & ((pad_row == 1) | (rows == cols))


def attention_kernel(seg_row, seg_col, pad_row, q, k, v, o):
    allowed = allowed_mask(seg_row[...], seg_col[...], pad_row[...])
    for h in range(q.shape[1] // HEAD):
        at = slice(h * HEAD, (h + 1) * HEAD)
        p = scores(q[:, at], k[:, at], allowed)
        o[:, at] = dot_nn(p.astype(BF), v[:, at]).astype(BF)


def attention(masks, q, k, v):
    rows, width = q.shape
    full = pl.BlockSpec(memory_space=pltpu.VMEM)
    return pl.pallas_call(
        attention_kernel,
        in_specs=[full] * 6,
        out_specs=full,
        out_shape=jax.ShapeDtypeStruct((rows, width), BF),
        compiler_params=pltpu.CompilerParams(vmem_limit_bytes=32 * 1024 * 1024),
        cost_estimate=pl.CostEstimate(
            flops=4 * rows * rows * width,
            bytes_accessed=8 * rows * width,
            transcendentals=rows * rows * width // HEAD,
        ),
    )(*masks, q, k, v)


def attention_back_kernel(seg_row, seg_col, pad_row, q, k, v, do, dq, dk, dv):
    allowed = allowed_mask(seg_row[...], seg_col[...], pad_row[...])
    for h in range(q.shape[1] // HEAD):
        at = slice(h * HEAD, (h + 1) * HEAD)
        p = scores(q[:, at], k[:, at], allowed)
        dp = dot_nt(do[:, at], v[:, at])
        delta = jnp.sum(dp * p, axis=-1, keepdims=True)
        ds = (p * (dp - delta)).astype(BF)
        dq[:, at] = (dot_nn(ds, k[:, at]) * score_scale).astype(BF)
        dk[:, at] = (dot_tn(ds, q[:, at]) * score_scale).astype(BF)
        dv[:, at] = dot_tn(p.astype(BF), do[:, at]).astype(BF)


def attention_back(masks, q, k, v, do):
    rows, width = q.shape
    full = pl.BlockSpec(memory_space=pltpu.VMEM)
    return pl.pallas_call(
        attention_back_kernel,
        in_specs=[full] * 7,
        out_specs=[full] * 3,
        out_shape=[jax.ShapeDtypeStruct((rows, width), BF)] * 3,
        compiler_params=pltpu.CompilerParams(vmem_limit_bytes=32 * 1024 * 1024),
        cost_estimate=pl.CostEstimate(
            flops=10 * rows * rows * width,
            bytes_accessed=14 * rows * width,
            transcendentals=rows * rows * width // HEAD,
        ),
    )(*masks, q, k, v, do)


def expert_kernel(
    n_exp,
    n_ff,
    has_sum,
    h2,
    cot,
    place,
    weight,
    mask,
    w_gate,
    w_up,
    w_low,
    d_gu,
    l_gate,
    l_up,
    d_low,
    l_low,
    *refs,
):
    if has_sum:
        refs = refs[5:]
    (out, dh2, g_gu, g_lg, g_lu, g_dl, g_ll) = refs[:7]
    (x_s, dy_s, rgu_s, drl_s, sw_s, y_acc, dx_acc, rl_acc, drgu_acc, sel, y_all, dx_all) = refs[7:]
    e = pl.program_id(0)
    f = pl.program_id(1)
    keep = mask[...]
    keep_one = keep[:, :PACK]
    base = pl.multiple_of(e * MOST, MOST)

    @pl.when(f == 0)
    def _():
        slots = lax.broadcasted_iota(jnp.int32, (MOST, place.shape[2]), 0)
        hit = slots == place[0]
        pick = jnp.where(hit, 1.0, 0.0).astype(BF)
        sel[pl.ds(base, MOST), :] = pick
        sw = jnp.sum(jnp.where(hit, weight[0], 0.0), axis=1, keepdims=True)
        sw_s[...] = sw
        x = dot_nn(pick, h2[...]).astype(BF)
        dy = (dot_nn(pick, cot[...]) * sw).astype(BF)
        x_s[...] = x
        dy_s[...] = dy
        rgu_s[...] = (dot_nt(x, d_gu[0]) * keep).astype(BF)
        drl_s[...] = (adapter_scale * dot_nt(dy, l_low[0]) * keep_one).astype(BF)
        y_acc[...] = jnp.zeros_like(y_acc)
        dx_acc[...] = jnp.zeros_like(dx_acc)
        rl_acc[...] = jnp.zeros_like(rl_acc)
        drgu_acc[...] = jnp.zeros_like(drgu_acc)

    x = x_s[...]
    dy = dy_s[...]
    r_g = rgu_s[:, :PACK]
    r_u = rgu_s[:, PACK:]
    gate = dot_nn(x, w_gate[0]) + adapter_scale * dot_nn(r_g, l_gate[0])
    up = dot_nn(x, w_up[0]) + adapter_scale * dot_nn(r_u, l_up[0])
    sig = 1.0 / (1.0 + jnp.exp(-gate))
    act = gate * sig
    hidden = (act * up).astype(BF)
    rl_acc[...] += dot_nt(hidden, d_low[0])
    y_acc[...] += dot_nn(hidden, w_low[0])
    d_hidden = dot_nt(dy, w_low[0]) + dot_nn(drl_s[...], d_low[0])
    d_gate = (d_hidden * up * sig * (1.0 + gate * (1.0 - sig))).astype(BF)
    d_up = (d_hidden * act).astype(BF)
    drgu_acc[:, :PACK] += dot_nt(d_gate, l_gate[0])
    drgu_acc[:, PACK:] += dot_nt(d_up, l_up[0])
    dx_acc[...] += dot_nt(d_gate, w_gate[0]) + dot_nt(d_up, w_up[0])
    g_lg[0] = adapter_scale * dot_tn(r_g, d_gate)
    g_lu[0] = adapter_scale * dot_tn(r_u, d_up)
    g_dl[0] = dot_tn(drl_s[...], hidden)

    @pl.when(f == n_ff - 1)
    def _():
        x = x_s[...]
        dy = dy_s[...]
        r_low = (rl_acc[...] * keep_one).astype(BF)
        y = y_acc[...] + adapter_scale * dot_nn(r_low, l_low[0])
        y_all[pl.ds(base, MOST), :] = (y * sw_s[...]).astype(BF)
        dr = (adapter_scale * drgu_acc[...] * keep).astype(BF)
        dx_all[pl.ds(base, MOST), :] = (dx_acc[...] + dot_nn(dr, d_gu[0])).astype(BF)
        g_ll[0] = adapter_scale * dot_tn(r_low, dy)
        g_gu[0] = dot_tn(dr, x)

    @pl.when((f == n_ff - 1) & (e == n_exp - 1))
    def _():
        out[...] = dot_tn(sel[...], y_all[...]).astype(out.dtype)
        dh2[...] = dot_tn(sel[...], dx_all[...]).astype(dh2.dtype)


def expert_chunk(h2, cot, place, weight, mask, params, out_type, ff_block=512):
    w_gate, w_up, w_low, d_gu, l_gate, l_up, d_low, l_low = params
    n_exp, width, ff = w_gate.shape
    rows = h2.shape[0]
    n_ff = ff // ff_block
    whole = lambda e, f: (0, 0)
    per_e = lambda e, f: (e, 0, 0)
    cols = lambda e, f: (e, 0, f)
    grads = [
        (2 * PACK, width, per_e, width),
        (PACK, ff, cols, ff_block),
        (PACK, ff, cols, ff_block),
        (PACK, ff, cols, ff_block),
        (PACK, width, per_e, width),
    ]
    return pl.pallas_call(
        functools.partial(expert_kernel, n_exp, n_ff, False),
        grid=(n_exp, n_ff),
        in_specs=[
            pl.BlockSpec((rows, width), whole),
            pl.BlockSpec((rows, width), whole),
            pl.BlockSpec((1, 1, rows), per_e),
            pl.BlockSpec((1, 1, rows), per_e),
            pl.BlockSpec((1, 2 * PACK), whole),
            pl.BlockSpec((1, width, ff_block), cols),
            pl.BlockSpec((1, width, ff_block), cols),
            pl.BlockSpec((1, ff_block, width), lambda e, f: (e, f, 0)),
            pl.BlockSpec((1, 2 * PACK, width), per_e),
            pl.BlockSpec((1, PACK, ff_block), cols),
            pl.BlockSpec((1, PACK, ff_block), cols),
            pl.BlockSpec((1, PACK, ff_block), cols),
            pl.BlockSpec((1, PACK, width), per_e),
        ],
        out_specs=[
            pl.BlockSpec((rows, width), whole),
            pl.BlockSpec((rows, width), whole),
        ]
        + [pl.BlockSpec((1, g[0], g[3]), g[2]) for g in grads],
        out_shape=[
            jax.ShapeDtypeStruct((rows, width), out_type),
            jax.ShapeDtypeStruct((rows, width), out_type),
        ]
        + [jax.ShapeDtypeStruct((n_exp, g[0], g[1]), F32) for g in grads],
        scratch_shapes=[
            pltpu.VMEM((MOST, width), BF),
            pltpu.VMEM((MOST, width), BF),
            pltpu.VMEM((MOST, 2 * PACK), BF),
            pltpu.VMEM((MOST, PACK), BF),
            pltpu.VMEM((MOST, 1), F32),
            pltpu.VMEM((MOST, width), F32),
            pltpu.VMEM((MOST, width), F32),
            pltpu.VMEM((MOST, PACK), F32),
            pltpu.VMEM((MOST, 2 * PACK), F32),
            pltpu.VMEM((n_exp * MOST, rows), BF),
            pltpu.VMEM((n_exp * MOST, width), BF),
            pltpu.VMEM((n_exp * MOST, width), BF),
        ],
        compiler_params=pltpu.CompilerParams(
            vmem_limit_bytes=VMEM, dimension_semantics=("arbitrary", "arbitrary")
        ),
        cost_estimate=pl.CostEstimate(
            flops=20 * n_exp * MOST * width * ff,
            bytes_accessed=6 * n_exp * width * ff,
            transcendentals=n_exp * MOST * ff,
        ),
    )(h2, cot, place, weight, mask, w_gate, w_up, w_low, d_gu, l_gate, l_up, d_low, l_low)


def local(
    n_rep,
    n_shard,
    tokens,
    cotangent,
    segments,
    padding,
    routes,
    route_weights,
    adapter_set,
    norm_one,
    norm_two,
    query_weight,
    key_weight,
    value_weight,
    output_weight,
    query_down,
    key_down,
    value_down,
    output_down,
    query_lift,
    key_lift,
    value_lift,
    output_lift,
    expert_gate,
    expert_upper,
    expert_lower,
    gate_down,
    gate_lift,
    upper_down,
    upper_lift,
    lower_down,
    lower_lift,
):
    seq_len, width = tokens.shape
    n_exp = expert_gate.shape[0]
    cols = query_weight.shape[1]
    team = min(cols // HEAD, n_rep // 2)
    half = width // 2
    plane = lax.axis_index("shard")
    rep = lax.axis_index("rep")
    core = rep % 2
    chip = (rep // 2) % team

    def rep_swap(x, bits):
        return lax.ppermute(x, "rep", [(a, a ^ bits) for a in range(n_rep)])

    def line_gather(x):
        from_up, from_down = [x], [x]
        for _ in range(1, n_shard):
            from_up.append(
                lax.ppermute(from_up[-1], "shard", [(a, a - 1) for a in range(1, n_shard)])
            )
            from_down.append(
                lax.ppermute(from_down[-1], "shard", [(a, a + 1) for a in range(n_shard - 1)])
            )
        return [x] + [from_up[k] + from_down[n_shard - k] for k in range(1, n_shard)]

    def line_send(x, k):
        return lax.ppermute(x, "shard", [(a, (a + k) % n_shard) for a in range(n_shard)])

    def in_order(parts):
        return jnp.roll(jnp.stack(parts), plane, axis=0)

    def chip_gather(x):
        return [x] + [rep_swap(x, j << 1) for j in range(1, team)]

    def flat(table):
        return table.reshape(table.shape[0], PACK).T

    packed = jnp.concatenate(
        [
            flat(t)
            for t in (
                query_down,
                key_down,
                value_down,
                output_down,
                query_lift,
                key_lift,
                value_lift,
                output_lift,
            )
        ],
        axis=0,
    )
    groups = 2 * team
    group = chip * 2 + core
    pack_rows = 8 * PACK // groups
    pack_own = lax.dynamic_slice(packed, (group * pack_rows, 0), (pack_rows, cols))
    pack_line = in_order(line_gather(pack_own))
    pack_line = pack_line.transpose(1, 0, 2).reshape(pack_rows, width)
    pack_same = jnp.stack(chip_gather(pack_line))
    pack_other = rep_swap(pack_same, 1)
    pack_all = jnp.stack([pack_same, pack_other], axis=1).reshape(groups, pack_rows, width)
    pack_all = jnp.take(pack_all, jnp.arange(groups) ^ group, axis=0).reshape(8, PACK, width)
    downs, lifts = pack_all[:4], pack_all[4:]

    def own_block(weight):
        block = lax.dynamic_slice(weight, (core * half, chip * HEAD), (half, HEAD))
        block = in_order(line_gather(block))
        return block.transpose(1, 0, 2).reshape(half, n_shard * HEAD)

    def share(block):
        same = chip_gather(block)
        return same, [rep_swap(b, 1) for b in same]

    blocks = [share(own_block(w)) for w in (query_weight, key_weight, value_weight)]
    out_rows = output_weight.reshape(2, n_shard // 2, cols // HEAD, HEAD, cols)
    out_own = lax.dynamic_slice(
        out_rows, (core, 0, chip, 0, 0), (1, n_shard // 2, 1, HEAD, cols)
    ).reshape(n_shard // 2 * HEAD, cols)
    out_own = in_order(line_gather(out_own)).transpose(1, 0, 2).reshape(-1, width)
    out_same, out_other = share(out_own)

    def chip_cols(table, j):
        parts = table.reshape(table.shape[0], n_shard, team, HEAD)
        return lax.dynamic_index_in_dim(parts, chip ^ j, 2, keepdims=False).reshape(
            table.shape[0], n_shard * HEAD
        )

    def pick_half(x, which):
        size = x.shape[1] // 2
        return lax.dynamic_slice(x, (0, which * size), (x.shape[0], size))

    chosen_set = adapter_set[0]
    set_flags = (jnp.arange(SETS, dtype=jnp.int32) == chosen_set).astype(F32)
    keep = jnp.repeat(set_flags, RANK)[None]
    masks = (segments, segments.reshape(seq_len, 1), padding)
    residual = tokens.astype(F32)
    normed_one = rms_forward(residual, norm_one).astype(BF)
    near, far = pick_half(normed_one, core), pick_half(normed_one, 1 - core)
    reduced = [(dot_nt(normed_one, downs[a]) * keep).astype(BF) for a in range(3)]

    def project(a, j):
        same, other = blocks[a]
        y = dot_nn(near, same[j]) + dot_nn(far, other[j])
        y = y + adapter_scale * dot_nn(reduced[a], chip_cols(lifts[a], j))
        return y.astype(BF)

    heads = [[project(a, j) for a in range(3)] for j in range(team)]
    mixed = [attention(masks, *heads[j]) for j in range(team)]
    reduced_out = sum(dot_nt(mixed[j], chip_cols(downs[3], j)) for j in range(team))
    reduced_out = (reduced_out * keep).astype(BF)
    attn_out = adapter_scale * dot_nn(reduced_out, lifts[3])
    for j in range(team):
        attn_out = attn_out + dot_nn(pick_half(mixed[j], core), out_same[j])
        attn_out = attn_out + dot_nn(pick_half(mixed[j], 1 - core), out_other[j])
    after_attn = residual + attn_out
    normed_two = rms_forward(after_attn, norm_two).astype(BF)

    expert_ids = jnp.arange(EXPERTS, dtype=jnp.int32)
    picked = routes[:, :, None] == expert_ids[None, None, :]
    member = jnp.sum(picked.astype(jnp.int32), axis=1)
    before = jnp.cumsum(member, axis=0) - member
    place = jnp.where(member == 1, before, -1).T
    per_expert = jnp.sum(jnp.where(picked, route_weights[:, :, None], 0.0), axis=1).T
    info = jnp.concatenate(
        [
            place.astype(F32),
            per_expert,
            jnp.broadcast_to(chosen_set.astype(F32), (8, seq_len)),
        ],
        axis=0,
    )
    info_line = line_gather(info)
    cot_line = line_gather(cotangent)
    rows_line = line_gather(normed_two)
    params = (
        expert_gate,
        expert_upper,
        expert_lower,
        jnp.concatenate(
            [t.reshape(n_exp, width, PACK).transpose(0, 2, 1) for t in (gate_down, upper_down)],
            axis=1,
        ),
        gate_lift.reshape(n_exp, -1, PACK).transpose(0, 2, 1),
        upper_lift.reshape(n_exp, -1, PACK).transpose(0, 2, 1),
        lower_down.reshape(n_exp, -1, PACK).transpose(0, 2, 1),
        lower_lift.reshape(n_exp, width, PACK).transpose(0, 2, 1),
    )

    def chunk(k):
        line = info_line[k]
        at = plane * n_exp
        spot = lax.dynamic_slice(line, (at, 0), (n_exp, seq_len)).astype(jnp.int32)
        share_of = lax.dynamic_slice(line, (EXPERTS + at, 0), (n_exp, seq_len))
        row_set = line[2 * EXPERTS, 0].astype(jnp.int32)
        flags = (jnp.arange(SETS, dtype=jnp.int32) == row_set).astype(F32)
        mask = jnp.tile(jnp.repeat(flags, RANK), 2)[None]
        return expert_chunk(
            rows_line[k],
            cot_line[k],
            spot[:, None, :],
            share_of[:, None, :],
            mask,
            params,
            F32 if k == 0 else BF,
        )

    order = sorted(range(n_shard), key=lambda k: (k != 0, abs(2 * k - n_shard), k))
    results = {k: chunk(k) for k in order}
    dh2 = results[0][1]
    for k in order[1:]:
        dh2 = dh2 + line_send(results[k][1], k).astype(F32)
    output = after_attn + results[0][0]
    for k in order[1:]:
        output = output + line_send(results[k][0], k).astype(F32)
    output = output.astype(BF)
    expert_sums = [sum(results[k][2 + a] for k in order) for a in range(5)]
    expert_flat = jnp.concatenate(
        [g.astype(BF).reshape(-1, width) for g in expert_sums], axis=0
    )
    expert_flat = lax.psum(expert_flat, "rep")

    grad_after = cotangent.astype(F32)
    grad_mid = grad_after + rms_backward(after_attn, norm_two, dh2)
    grad_attn = grad_mid.astype(BF)
    d_reduced_out = (adapter_scale * dot_nt(grad_attn, lifts[3]) * keep).astype(BF)
    grad_out_lift = adapter_scale * dot_tn(reduced_out, grad_attn)

    def halves(a, b):
        return jnp.where(
            core == 0, jnp.concatenate([a, b], axis=1), jnp.concatenate([b, a], axis=1)
        )

    def grad_heads(j):
        g = halves(dot_nt(grad_attn, out_same[j]), dot_nt(grad_attn, out_other[j]))
        return (g + dot_nn(d_reduced_out, chip_cols(downs[3], j))).astype(BF)

    back = [attention_back(masks, *heads[j], grad_heads(j)) for j in range(team)]

    def from_chips(parts):
        stacked = jnp.stack([p.reshape(p.shape[0], n_shard, HEAD) for p in parts])
        stacked = jnp.take(stacked, jnp.arange(team) ^ chip, axis=0)
        return stacked.transpose(1, 2, 0, 3).reshape(parts[0].shape[0], width)

    down_grads, lift_grads = [], []
    near_grad = jnp.zeros((seq_len, half), F32)
    far_grad = jnp.zeros((seq_len, half), F32)
    low_grad = jnp.zeros((seq_len, width), F32)
    for a in range(3):
        dr = sum(dot_nt(back[j][a], chip_cols(lifts[a], j)) for j in range(team))
        dr = (adapter_scale * dr * keep).astype(BF)
        lift_grads.append(
            from_chips([adapter_scale * dot_tn(reduced[a], back[j][a]) for j in range(team)])
        )
        down_grads.append(dot_tn(dr, normed_one))
        low_grad = low_grad + dot_nn(dr, downs[a])
        for j in range(team):
            near_grad = near_grad + dot_nt(back[j][a], blocks[a][0][j])
            far_grad = far_grad + dot_nt(back[j][a], blocks[a][1][j])
    down_grads.append(from_chips([dot_tn(d_reduced_out, mixed[j]) for j in range(team)]))
    lift_grads.append(grad_out_lift)
    grad_normed_one = low_grad + halves(near_grad, far_grad)
    input_grad = (grad_mid + rms_backward(residual, norm_one, grad_normed_one)).astype(BF)
    attn_flat = jnp.stack(down_grads + lift_grads).astype(BF)
    attn_flat = attn_flat.reshape(8 * PACK, n_shard, cols).transpose(1, 0, 2)
    attn_flat = lax.psum_scatter(attn_flat, "shard", scatter_dimension=0, tiled=True)
    attn_flat = lax.psum(attn_flat.reshape(8 * PACK, cols), "rep").astype(F32)

    def unflat(g):
        return g.T.reshape(cols, SETS, RANK)

    attn_outs = [unflat(attn_flat[a * PACK : (a + 1) * PACK]) for a in range(8)]

    ff = expert_gate.shape[2]
    sizes = [(2 * PACK, width), (PACK, ff), (PACK, ff), (PACK, ff), (PACK, width)]
    parts, start = [], 0
    for height, long in sizes:
        count = n_exp * height * long // width
        parts.append(expert_flat[start : start + count].astype(F32).reshape(n_exp, height, long))
        start += count

    def restore(g):
        return g.transpose(0, 2, 1).reshape(n_exp, -1, SETS, RANK)

    expert_outs = [
        restore(parts[0][:, :PACK]),
        restore(parts[1]),
        restore(parts[0][:, PACK:]),
        restore(parts[2]),
        restore(parts[3]),
        restore(parts[4]),
    ]
    return (output, input_grad, *attn_outs, *expert_outs)


def solution(mesh):
    rows = P(("rep", "shard"), None)
    second = P(None, "shard")
    three = P("shard", None, None)
    four = P("shard", None, None, None)
    placed = (rows,) * 6 + (P(("rep", "shard")), P(), P()) + (second,) * 4
    placed = placed + (three,) * 11 + (four,) * 6
    return jax.shard_map(
        functools.partial(local, mesh.shape["rep"], mesh.shape["shard"]),
        mesh=mesh,
        in_specs=placed,
        out_specs=(rows, rows) + (three,) * 8 + (four,) * 6,
        check_vma=False,
    )
```

```python
import functools

import jax
import jax.numpy as jnp
from jax import lax
from jax.experimental import pallas as pl
from jax.experimental.pallas import tpu as pltpu
from jax.sharding import PartitionSpec as P

HEADS = 16
HEAD = 128
TOP = 8
EXPERTS = 16
RANK = 16
SETS = 2
MOST = 160
PACK = SETS * RANK

epsilon = 1e-06
adapter_scale = 2.0
masked_score = -1e30
score_scale = HEAD ** (-0.5)

BF = jnp.bfloat16
F32 = jnp.float32
VMEM = 56 * 1024 * 1024


def dot_nn(a, b):
    return jnp.dot(a, b, preferred_element_type=F32)


def dot_nt(a, b):
    return lax.dot_general(a, b, (((1,), (1,)), ((), ())), preferred_element_type=F32)


def dot_tn(a, b):
    return lax.dot_general(a, b, (((0,), (0,)), ((), ())), preferred_element_type=F32)


def rms_forward(values, gain_vec):
    inverse = lax.rsqrt(jnp.mean(values * values, axis=-1, keepdims=True) + epsilon)
    return values * inverse * gain_vec


def rms_backward(values, gain_vec, grad_norm):
    inverse = lax.rsqrt(jnp.mean(values * values, axis=-1, keepdims=True) + epsilon)
    weighted = grad_norm * gain_vec
    cubed = inverse * inverse * inverse
    return inverse * weighted - values * cubed * jnp.mean(values * weighted, axis=-1, keepdims=True)


def scores(q, k, allowed):
    s = dot_nt(q, k) * score_scale
    s = jnp.where(allowed, s, masked_score)
    e = jnp.exp(s - jnp.max(s, axis=-1, keepdims=True))
    return e / jnp.sum(e, axis=-1, keepdims=True)


def allowed_mask(seg_row, seg_col, pad_row):
    shape = (seg_col.shape[0], seg_row.shape[1])
    rows = lax.broadcasted_iota(jnp.int32, shape, 0)
    cols = lax.broadcasted_iota(jnp.int32, shape, 1)
    return (seg_col == seg_row) & ((pad_row == 1) | (rows == cols))


def project_kernel(sizes, ids, h, flags, near1, near2, far1, far2, downs, lifts, *refs):
    team, n_line, rows, width = sizes
    outs, (r_own, w_s, r_s) = refs[:team], refs[team:]
    core = ids[2]
    half = width // 2
    span = n_line * HEAD
    here = pl.multiple_of(core * half, half)
    there = pl.multiple_of((1 - core) * half, half)
    for j in range(team):
        at = slice(j * rows, (j + 1) * rows)
        keep = flags[j, :1, : 3 * PACK].astype(F32)
        r_s[at, :] = (dot_nt(h[at, :], downs[: 3 * PACK, :]) * keep).astype(BF)
    for a in range(3):
        r_own[a] = r_s[:rows, a * PACK : (a + 1) * PACK]
    for a, (near, far, start) in enumerate(((near1, far1, 0), (near2, far2, 0), (near2, far2, half))):
        for z in range(n_line):
            at = slice(z * HEAD, (z + 1) * HEAD)
            w_s[a, pl.ds(here, half), at] = near[z, start : start + half, :]
            w_s[a, pl.ds(there, half), at] = far[z, start : start + half, :]
    tile = min(256, span)
    per = span // tile

    def step(i, carry):
        a = i // per
        at = pl.multiple_of((i % per) * tile, tile)
        y = dot_nn(h[...], w_s[a, :, pl.ds(at, tile)])
        y = y + adapter_scale * dot_nn(r_s[...], lifts[a, :, pl.ds(at, tile)])
        y = y.astype(BF)
        for j in range(team):
            outs[j][:, pl.ds(pl.multiple_of(i * tile, tile), tile)] = y[j * rows : (j + 1) * rows]
        return carry

    lax.fori_loop(0, 3 * per, step, 0)


def project(ids, h, flags, near, far, downs, lifts, sizes):
    team, n_line, rows, width = sizes
    span = n_line * HEAD
    full = pl.BlockSpec(memory_space=pltpu.VMEM)
    got = pl.pallas_call(
        functools.partial(project_kernel, sizes),
        in_specs=[pl.BlockSpec(memory_space=pltpu.SMEM)] + [full] * 8,
        out_specs=[full] * (team + 1),
        out_shape=[jax.ShapeDtypeStruct((rows, 3 * span), BF)] * team
        + [jax.ShapeDtypeStruct((3, rows, PACK), BF)],
        scratch_shapes=[
            pltpu.VMEM((3, width, span), BF),
            pltpu.VMEM((team * rows, 3 * PACK), BF),
        ],
        compiler_params=pltpu.CompilerParams(vmem_limit_bytes=VMEM),
        cost_estimate=pl.CostEstimate(
            flops=6 * team * rows * width * span, bytes_accessed=12 * width * span, transcendentals=0
        ),
    )(ids, h, flags, *near, *far, downs, lifts)
    return got[:team], got[team]


def chip_columns(ref, chip, n_line, cols):
    parts = []
    for z in range(n_line):
        parts.append(ref[:, pl.ds(pl.multiple_of(z * cols + chip * HEAD, HEAD), HEAD)])
    return jnp.concatenate(parts, axis=1)


def mix_kernel(sizes, ids, seg_row, seg_col, pad_row, tokens, gain, d_out, l_out, keep, *refs):
    team, n_line, rows, width, cols = sizes
    qkv, refs = refs[:team], refs[team:]
    near, refs = refs[:team], refs[team:]
    far, refs = refs[:team], refs[team:]
    mixed, r_out, x1, h2, acc = refs
    chip, core = ids[1], ids[2]
    span = n_line * HEAD
    side = span // 2
    allowed = allowed_mask(seg_row[...], seg_col[...], pad_row[...])
    reduced = jnp.zeros((rows, PACK), F32)
    for j in range(team):
        for z in range(n_line):
            q, k, v = (
                qkv[j][:, a * span + z * HEAD : a * span + (z + 1) * HEAD] for a in range(3)
            )
            p = scores(q, k, allowed)
            mixed[:, j * span + z * HEAD : j * span + (z + 1) * HEAD] = dot_nn(
                p.astype(BF), v
            ).astype(BF)
        o = mixed[:, j * span : (j + 1) * span]
        reduced = reduced + dot_nt(o, chip_columns(d_out, chip ^ j, n_line, cols))
        mine = mixed[:, pl.ds(pl.multiple_of(j * span + core * side, HEAD), side)]
        other = mixed[:, pl.ds(pl.multiple_of(j * span + (1 - core) * side, HEAD), side)]
        part = dot_nn(mine, near[j][...]) + dot_nn(other, far[j][...])
        if j == 0:
            acc[...] = part
        else:
            acc[...] += part
    low = (reduced * keep[...]).astype(BF)
    r_out[...] = low
    total = tokens[...].astype(F32) + (acc[...] + adapter_scale * dot_nn(low, l_out[...]))
    x1[...] = total
    h2[...] = rms_forward(total, gain[...]).astype(BF)


def mix(ids, masks, tokens, gain, d_out, l_out, keep, qkv, near, far, sizes):
    team, n_line, rows, width, cols = sizes
    full = pl.BlockSpec(memory_space=pltpu.VMEM)
    return pl.pallas_call(
        functools.partial(mix_kernel, sizes),
        in_specs=[pl.BlockSpec(memory_space=pltpu.SMEM)] + [full] * (8 + 3 * team),
        out_specs=[full] * 4,
        out_shape=[
            jax.ShapeDtypeStruct((rows, width), BF),
            jax.ShapeDtypeStruct((rows, PACK), BF),
            jax.ShapeDtypeStruct((rows, width), F32),
            jax.ShapeDtypeStruct((rows, width), BF),
        ],
        scratch_shapes=[pltpu.VMEM((rows, width), F32)],
        compiler_params=pltpu.CompilerParams(vmem_limit_bytes=VMEM),
        cost_estimate=pl.CostEstimate(
            flops=2 * rows * width * width + 4 * rows * rows * width,
            bytes_accessed=2 * width * width + 12 * rows * width,
            transcendentals=rows * rows * HEADS,
        ),
    )(ids, *masks, tokens, gain, d_out, l_out, keep, *qkv, *near, *far)


def back_kernel(sizes, ids, *refs):
    team, n_line, rows, width, cols = sizes
    (seg_row, seg_col, pad_row, tokens, cot, x1, gain1, gain2, own, downs, l_out, keep) = refs[:12]
    refs = refs[12:]
    parts, refs = refs[: n_line - 1], refs[n_line - 1 :]
    mixed, r_own, r_out = refs[:3]
    refs = refs[3:]
    qkv, refs = refs[:team], refs[team:]
    near_o, refs = refs[:team], refs[team:]
    far_o, refs = refs[:team], refs[team:]
    weights, in_grad, grads, near_s, far_s, sems, dx1_s, da_s, do_s, do_b, dp_s, acc, h1_s, dr, lift_s = refs
    chip, core = ids[1], ids[2]
    span = n_line * HEAD
    side = span // 2
    half = width // 2
    lift_gap = 3 * PACK // 2
    lift_end = half + lift_gap
    slots = near_s.shape[0]

    def fetch(j):
        copies = []
        for side_at, buf in ((core, near_s), (1 - core, far_s)):
            source = ids[3] + (chip ^ j) * 2 + side_at
            number = 0 if buf is near_s else 1
            for z in range(n_line):
                copies.append(
                    pltpu.make_async_copy(
                        weights.at[source, z],
                        buf.at[j % slots, :, z * HEAD : (z + 1) * HEAD],
                        sems.at[j % slots, number, z],
                    )
                )
        return copies

    for copy in fetch(0):
        copy.start()
    mask = keep[...]
    dh2 = own[...]
    for part in parts:
        dh2 = dh2 + part[...].astype(F32)
    dx1 = cot[...].astype(F32) + rms_backward(x1[...], gain2[...], dh2)
    dx1_s[...] = dx1
    da_s[...] = dx1.astype(BF)
    h1_s[...] = rms_forward(tokens[...].astype(F32), gain1[...]).astype(BF)
    da = da_s[...]
    d_low = (adapter_scale * dot_nt(da, l_out[...]) * mask).astype(BF)

    def put_all(row, block):
        for z in range(n_line):
            grads[z, row : row + PACK, :] = block[:, z * cols : (z + 1) * cols].astype(BF)

    put_all(7 * PACK, adapter_scale * dot_tn(r_out[...], da))
    allowed = allowed_mask(seg_row[...], seg_col[...], pad_row[...])
    dr[...] = jnp.zeros_like(dr)
    here = pl.multiple_of(core * half, half)
    there = pl.multiple_of((1 - core) * half, half)
    acc[...] = jnp.zeros_like(acc)
    for j in range(team):
        ahead = j + slots - 1
        if 0 < ahead < team:
            for copy in fetch(ahead):
                copy.start()
        spot = chip ^ j

        def put(row, block):
            for z in range(n_line):
                at = pl.multiple_of(spot * HEAD, HEAD)
                grads[z, pl.ds(row, PACK), pl.ds(at, HEAD)] = block[
                    :, z * HEAD : (z + 1) * HEAD
                ].astype(BF)

        do_s[:, pl.ds(pl.multiple_of(core * side, HEAD), side)] = dot_nt(da, near_o[j][...])
        do_s[:, pl.ds(pl.multiple_of((1 - core) * side, HEAD), side)] = dot_nt(da, far_o[j][...])
        do = do_s[...] + dot_nn(
            d_low, chip_columns(downs.at[3 * PACK :, :], spot, n_line, cols)
        )
        do = do.astype(BF)
        put(3 * PACK, dot_tn(d_low, mixed[:, j * span : (j + 1) * span]))
        do_b[...] = do

        def head(z, carry):
            at = pl.multiple_of(z * HEAD, HEAD)
            q, k, v = (
                qkv[j][:, pl.ds(pl.multiple_of(a * span + at, HEAD), HEAD)] for a in range(3)
            )
            p = scores(q, k, allowed)
            do_h = do_b[:, pl.ds(at, HEAD)]
            dp = dot_nt(do_h, v)
            delta = jnp.sum(dp * p, axis=-1, keepdims=True)
            ds = (p * (dp - delta)).astype(BF)
            heads = (
                dot_nn(ds, k) * score_scale,
                dot_tn(ds, q) * score_scale,
                dot_tn(p.astype(BF), do_h),
            )
            for a in range(3):
                dp_s[:, pl.ds(pl.multiple_of(a * span + at, HEAD), HEAD)] = heads[a].astype(BF)
            return carry

        lax.fori_loop(0, n_line, head, 0, unroll=2)
        for copy in fetch(j):
            copy.wait()
        slot = j % slots
        packs = jnp.where(
            core == 0,
            jnp.concatenate([near_s[slot, half:lift_end, :], far_s[slot, half:lift_end, :]]),
            jnp.concatenate([far_s[slot, half:lift_end, :], near_s[slot, half:lift_end, :]]),
        )
        for a in range(3):
            lift_s[a] = packs[a * PACK : (a + 1) * PACK]

        def grad(a, carry):
            g = dp_s[:, pl.ds(pl.multiple_of(a * span, HEAD), span)]
            lift = lift_s[a]
            dr[a] += dot_nt(g, lift)
            put(
                pl.multiple_of((4 + a) * PACK, PACK), adapter_scale * dot_tn(r_own[a], g)
            )
            rows_a = pl.ds(pl.multiple_of(a * half + lift_gap * jnp.minimum(a, 1), 16), half)
            acc[:, pl.ds(here, half)] += dot_nt(g, near_s[slot, rows_a, :])
            acc[:, pl.ds(there, half)] += dot_nt(g, far_s[slot, rows_a, :])
            return carry

        lax.fori_loop(0, 3, grad, 0)
    h1 = h1_s[...]
    for a in range(3):
        low = (adapter_scale * dr[a] * mask).astype(BF)
        put_all(a * PACK, dot_tn(low, h1))
        acc[...] += dot_nn(low, downs[a * PACK : (a + 1) * PACK, :])
    total = dx1_s[...] + rms_backward(tokens[...].astype(F32), gain1[...], acc[...])
    in_grad[...] = total.astype(BF)


def attention_back(ids, small, parts, kept, qkv, near_o, far_o, weights, sizes):
    team, n_line, rows, width, cols = sizes
    span = n_line * HEAD
    full = pl.BlockSpec(memory_space=pltpu.VMEM)
    count = len(small) + len(parts) + len(kept) + 3 * team
    slots = 2 if span <= 512 else 1
    return pl.pallas_call(
        functools.partial(back_kernel, sizes),
        in_specs=[pl.BlockSpec(memory_space=pltpu.SMEM)]
        + [full] * count
        + [pl.BlockSpec(memory_space=pl.ANY)],
        out_specs=[full] * 2,
        out_shape=[
            jax.ShapeDtypeStruct((rows, width), BF),
            jax.ShapeDtypeStruct((n_line, 8 * PACK, cols), BF),
        ],
        scratch_shapes=[
            pltpu.VMEM((slots, weights.shape[2], span), BF),
            pltpu.VMEM((slots, weights.shape[2], span), BF),
            pltpu.SemaphoreType.DMA((slots, 2, n_line)),
            pltpu.VMEM((rows, width), F32),
            pltpu.VMEM((rows, width), BF),
            pltpu.VMEM((rows, span), F32),
            pltpu.VMEM((rows, span), BF),
            pltpu.VMEM((rows, 3 * span), BF),
            pltpu.VMEM((rows, width), F32),
            pltpu.VMEM((rows, width), BF),
            pltpu.VMEM((3, rows, PACK), F32),
            pltpu.VMEM((3, PACK, span), BF),
        ],
        compiler_params=pltpu.CompilerParams(vmem_limit_bytes=VMEM),
        cost_estimate=pl.CostEstimate(
            flops=8 * rows * width * width + 10 * rows * rows * width,
            bytes_accessed=8 * width * width + 20 * rows * width,
            transcendentals=rows * rows * HEADS,
        ),
    )(ids, *small, *parts, *kept, *qkv, *near_o, *far_o, weights)


def expert_kernel(
    n_exp,
    n_ff,
    has_sum,
    source,
    h2,
    cot,
    place,
    weight,
    mask,
    w_gate,
    w_up,
    w_low,
    d_gu,
    l_gate,
    l_up,
    d_low,
    l_low,
    *refs,
):
    prior = (None,) * 5
    if has_sum:
        prior, refs = refs[:5], refs[5:]

    def emit(number, ref, value):
        if has_sum:
            value = value + prior[number][0].astype(F32)
        ref[0] = value.astype(ref.dtype)

    (out, dh2, g_gu, g_lg, g_lu, g_dl, g_ll) = refs[:7]
    (x_s, dy_s, rgu_s, drl_s, sw_s, y_acc, dx_acc, rl_acc, drgu_acc, sel, y_all, dx_all) = refs[7:]
    e = pl.program_id(0)
    f = pl.program_id(1)
    keep = mask[...]
    keep_one = keep[:, :PACK]
    base = pl.multiple_of(e * MOST, MOST)

    @pl.when(f == 0)
    def _():
        slots = lax.broadcasted_iota(jnp.int32, (MOST, place.shape[2]), 0)
        hit = slots == place[0]
        pick = jnp.where(hit, 1.0, 0.0).astype(BF)
        sel[pl.ds(base, MOST), :] = pick
        sw = jnp.sum(jnp.where(hit, weight[0], 0.0), axis=1, keepdims=True)
        sw_s[...] = sw
        x = dot_nn(pick, h2[...]).astype(BF)
        dy = (dot_nn(pick, cot[0]) * sw).astype(BF)
        x_s[...] = x
        dy_s[...] = dy
        rgu_s[...] = (dot_nt(x, d_gu[0]) * keep).astype(BF)
        drl_s[...] = (adapter_scale * dot_nt(dy, l_low[0]) * keep_one).astype(BF)
        y_acc[...] = jnp.zeros_like(y_acc)
        dx_acc[...] = jnp.zeros_like(dx_acc)
        rl_acc[...] = jnp.zeros_like(rl_acc)
        drgu_acc[...] = jnp.zeros_like(drgu_acc)

    x = x_s[...]
    dy = dy_s[...]
    r_g = rgu_s[:, :PACK]
    r_u = rgu_s[:, PACK:]
    gate = dot_nn(x, w_gate[0]) + adapter_scale * dot_nn(r_g, l_gate[0])
    up = dot_nn(x, w_up[0]) + adapter_scale * dot_nn(r_u, l_up[0])
    sig = 1.0 / (1.0 + jnp.exp(-gate))
    act = gate * sig
    hidden = (act * up).astype(BF)
    rl_acc[...] += dot_nt(hidden, d_low[0])
    y_acc[...] += dot_nn(hidden, w_low[0])
    d_hidden = dot_nt(dy, w_low[0]) + dot_nn(drl_s[...], d_low[0])
    d_gate = (d_hidden * up * sig * (1.0 + gate * (1.0 - sig))).astype(BF)
    d_up = (d_hidden * act).astype(BF)
    drgu_acc[:, :PACK] += dot_nt(d_gate, l_gate[0])
    drgu_acc[:, PACK:] += dot_nt(d_up, l_up[0])
    dx_acc[...] += dot_nt(d_gate, w_gate[0]) + dot_nt(d_up, w_up[0])
    emit(1, g_lg, adapter_scale * dot_tn(r_g, d_gate))
    emit(2, g_lu, adapter_scale * dot_tn(r_u, d_up))
    emit(3, g_dl, dot_tn(drl_s[...], hidden))

    @pl.when(f == n_ff - 1)
    def _():
        x = x_s[...]
        dy = dy_s[...]
        r_low = (rl_acc[...] * keep_one).astype(BF)
        y = y_acc[...] + adapter_scale * dot_nn(r_low, l_low[0])
        y_all[pl.ds(base, MOST), :] = (y * sw_s[...]).astype(BF)
        dr = (adapter_scale * drgu_acc[...] * keep).astype(BF)
        dx_all[pl.ds(base, MOST), :] = (dx_acc[...] + dot_nn(dr, d_gu[0])).astype(BF)
        emit(4, g_ll, adapter_scale * dot_tn(r_low, dy))
        emit(0, g_gu, dot_tn(dr, x))

    @pl.when((f == n_ff - 1) & (e == n_exp - 1))
    def _():
        out[...] = dot_tn(sel[...], y_all[...]).astype(out.dtype)
        dh2[...] = dot_tn(sel[...], dx_all[...]).astype(dh2.dtype)


def expert_chunk(source, h2, cot, place, weight, mask, params, prior, out_type, ff_block=512):
    w_gate, w_up, w_low, d_gu, l_gate, l_up, d_low, l_low = params
    n_exp, width, ff = w_gate.shape
    rows = h2.shape[0]
    n_ff = ff // ff_block
    whole = lambda e, f, s: (0, 0)
    per_e = lambda e, f, s: (e, 0, 0)
    cols = lambda e, f, s: (e, 0, f)
    grads = [
        (2 * PACK, width, per_e, width),
        (PACK, ff, cols, ff_block),
        (PACK, ff, cols, ff_block),
        (PACK, ff, cols, ff_block),
        (PACK, width, per_e, width),
    ]
    grad_specs = [pl.BlockSpec((1, g[0], g[3]), g[2]) for g in grads]
    grad_type = F32
    return pl.pallas_call(
        functools.partial(expert_kernel, n_exp, n_ff, prior is not None),
        grid_spec=pltpu.PrefetchScalarGridSpec(
            num_scalar_prefetch=1,
            grid=(n_exp, n_ff),
            in_specs=[
                pl.BlockSpec((rows, width), whole),
                pl.BlockSpec((1, rows, width), lambda e, f, s: (s[0], 0, 0)),
                pl.BlockSpec((1, 1, rows), per_e),
                pl.BlockSpec((1, 1, rows), per_e),
                pl.BlockSpec((1, 2 * PACK), whole),
                pl.BlockSpec((1, width, ff_block), cols),
                pl.BlockSpec((1, width, ff_block), cols),
                pl.BlockSpec((1, ff_block, width), lambda e, f, s: (e, f, 0)),
                pl.BlockSpec((1, 2 * PACK, width), per_e),
                pl.BlockSpec((1, PACK, ff_block), cols),
                pl.BlockSpec((1, PACK, ff_block), cols),
                pl.BlockSpec((1, PACK, ff_block), cols),
                pl.BlockSpec((1, PACK, width), per_e),
            ]
            + (grad_specs if prior is not None else []),
            out_specs=[
                pl.BlockSpec((rows, width), whole),
                pl.BlockSpec((rows, width), whole),
            ]
            + grad_specs,
            scratch_shapes=[
                pltpu.VMEM((MOST, width), BF),
                pltpu.VMEM((MOST, width), BF),
                pltpu.VMEM((MOST, 2 * PACK), BF),
                pltpu.VMEM((MOST, PACK), BF),
                pltpu.VMEM((MOST, 1), F32),
                pltpu.VMEM((MOST, width), F32),
                pltpu.VMEM((MOST, width), F32),
                pltpu.VMEM((MOST, PACK), F32),
                pltpu.VMEM((MOST, 2 * PACK), F32),
                pltpu.VMEM((n_exp * MOST, rows), BF),
                pltpu.VMEM((n_exp * MOST, width), BF),
                pltpu.VMEM((n_exp * MOST, width), BF),
            ],
        ),
        out_shape=[
            jax.ShapeDtypeStruct((rows, width), out_type),
            jax.ShapeDtypeStruct((rows, width), out_type),
        ]
        + [jax.ShapeDtypeStruct((n_exp, g[0], g[1]), grad_type) for g in grads],
        compiler_params=pltpu.CompilerParams(
            vmem_limit_bytes=VMEM, dimension_semantics=("arbitrary", "arbitrary")
        ),
        cost_estimate=pl.CostEstimate(
            flops=20 * n_exp * MOST * width * ff,
            bytes_accessed=6 * n_exp * width * ff,
            transcendentals=n_exp * MOST * ff,
        ),
    )(
        source,
        h2,
        cot,
        place,
        weight,
        mask,
        w_gate,
        w_up,
        w_low,
        d_gu,
        l_gate,
        l_up,
        d_low,
        l_low,
        *(prior or ()),
    )


def local(
    n_rep,
    n_shard,
    tokens,
    cotangent,
    segments,
    padding,
    routes,
    route_weights,
    adapter_set,
    norm_one,
    norm_two,
    query_weight,
    key_weight,
    value_weight,
    output_weight,
    query_down,
    key_down,
    value_down,
    output_down,
    query_lift,
    key_lift,
    value_lift,
    output_lift,
    expert_gate,
    expert_upper,
    expert_lower,
    gate_down,
    gate_lift,
    upper_down,
    upper_lift,
    lower_down,
    lower_lift,
):
    seq_len, width = tokens.shape
    n_exp, _, ff = expert_gate.shape
    cols = query_weight.shape[1]
    team = min(cols // HEAD, n_rep // 2)
    tiles = cols // HEAD
    half = width // 2
    plane = lax.axis_index("shard")
    rep = lax.axis_index("rep")
    core = rep % 2
    chip = (rep // 2) % team
    ids = jnp.stack([plane, chip, core, rep - rep % (2 * team)]).astype(jnp.int32)

    def rep_swap(x, bits):
        return lax.ppermute(x, "rep", [(a, a ^ bits) for a in range(n_rep)])

    def line_steps(x):
        from_up, from_down = [x], [x]
        for _ in range(1, n_shard):
            from_up.append(
                lax.ppermute(from_up[-1], "shard", [(a, a - 1) for a in range(1, n_shard)])
            )
            from_down.append(
                lax.ppermute(from_down[-1], "shard", [(a, a + 1) for a in range(n_shard - 1)])
            )
        return from_up, from_down

    def line_gather(x):
        up, down = line_steps(x)
        return [x] + [up[k] + down[n_shard - k] for k in range(1, n_shard)]

    def line_send(x, k):
        return lax.ppermute(x, "shard", [(a, (a + k) % n_shard) for a in range(n_shard)])

    def in_order(parts):
        buf = jnp.zeros((n_shard,) + parts[0].shape, parts[0].dtype)
        for k, part in enumerate(parts):
            buf = lax.dynamic_update_index_in_dim(buf, part, (plane + k) % n_shard, 0)
        return buf

    def chip_gather(x):
        return [x] + [rep_swap(x, j << 1) for j in range(1, team)]

    def after(x, *others):
        return lax.optimization_barrier((x,) + others)[0]

    chosen_set = adapter_set[0]
    set_flags = (jnp.arange(SETS, dtype=jnp.int32) == chosen_set).astype(F32)
    keep = jnp.repeat(set_flags, RANK)[None]
    masks = (segments, segments.reshape(seq_len, 1), padding)
    gain_one, gain_two = norm_one[None], norm_two[None]
    normed_one = rms_forward(tokens.astype(F32), gain_one).astype(BF)
    flag_rows = jnp.pad(jnp.tile(keep, (16, 3)), ((0, 0), (0, width - 3 * PACK))).astype(BF)
    sent_h = chip_gather(jnp.concatenate([normed_one, flag_rows], axis=0))
    flags = jnp.stack([h[seq_len:, :HEAD] for h in sent_h])
    hs = jnp.concatenate([h[:seq_len] for h in sent_h])

    def flat(table):
        return table.reshape(table.shape[0], PACK).T

    def pieces(x):
        return x.reshape(x.shape[0], tiles, HEAD).transpose(1, 0, 2).reshape(-1, HEAD)

    def whole_rows(x, height):
        x = x.reshape(n_shard, tiles, height, HEAD)
        return x.transpose(2, 0, 1, 3).reshape(height, width)

    def both(a, b, axis=0):
        return jnp.where(
            core == 0, jnp.concatenate([a, b], axis=axis), jnp.concatenate([b, a], axis=axis)
        )

    def slice_of(weight):
        return lax.dynamic_slice(weight, (core * half, chip * HEAD), (half, HEAD))

    def core_rows(table, height):
        return lax.dynamic_slice(table, (core * height, 0), (height, table.shape[1]))

    lift_rows = 3 * PACK // 2
    down_rows = 4 * PACK // 2
    last_rows = PACK // 2
    lift_pack = jnp.concatenate([flat(t) for t in (query_lift, key_lift, value_lift)], axis=0)
    down_pack = jnp.concatenate(
        [flat(t) for t in (query_down, key_down, value_down, output_down)], axis=0
    )
    out_rows = output_weight.reshape(2, n_shard // 2, tiles, HEAD, cols)
    out_own = lax.dynamic_slice(
        out_rows, (core, 0, chip, 0, 0), (1, n_shard // 2, 1, HEAD, cols)
    ).reshape(n_shard // 2 * HEAD, cols)
    first = [
        slice_of(query_weight),
        lax.dynamic_slice(lift_pack, (core * lift_rows, chip * HEAD), (lift_rows, HEAD)),
        pieces(core_rows(down_pack, down_rows)),
        pieces(core_rows(flat(output_lift), last_rows)),
        pieces(out_own),
    ]
    marks = [0]
    for piece in first:
        marks.append(marks[-1] + piece.shape[0])
    line1 = line_gather(jnp.concatenate(first, axis=0))
    near1 = in_order(line1)
    second = jnp.concatenate([slice_of(key_weight), slice_of(value_weight)], axis=0)
    line2 = line_gather(after(second, *line1, *sent_h))
    near2 = in_order(line2)
    far1 = rep_swap(near1[:, : marks[4]], 1)
    far2 = rep_swap(near2, 1)
    lifts = both(
        *(
            g[:, marks[1] : marks[2]].transpose(1, 0, 2).reshape(lift_rows, -1)
            for g in (near1, far1)
        )
    )
    lifts = jnp.stack(
        [
            jnp.pad(lifts[a * PACK : (a + 1) * PACK], ((a * PACK, (2 - a) * PACK), (0, 0)))
            for a in range(3)
        ]
    )
    downs = both(*(whole_rows(g[:, marks[2] : marks[3]], down_rows) for g in (near1, far1)))
    lift_out = both(*(whole_rows(g[:, marks[3] : marks[4]], last_rows) for g in (near1, far1)))
    out_block = whole_rows(near1[:, marks[4] :], n_shard // 2 * HEAD)
    near_o = chip_gather(out_block)
    far_o = [rep_swap(b, 1) for b in near_o]

    sizes = (team, n_shard, seq_len, width)
    made, r_own = project(ids, after(hs, *near_o), flags, (near1, near2), (far1, far2), downs, lifts, sizes)
    qkv = [made[0]] + [rep_swap(made[j], j << 1) for j in range(1, team)]
    sizes = sizes + (cols,)
    mixed, r_out, after_attn, normed_two = mix(
        ids, masks, tokens, gain_two, downs[3 * PACK :], lift_out, keep, qkv, near_o, far_o, sizes
    )

    expert_ids = jnp.arange(EXPERTS, dtype=jnp.int32)
    picked = routes[:, :, None] == expert_ids[None, None, :]
    member = jnp.sum(picked.astype(jnp.int32), axis=1)
    before = jnp.cumsum(member, axis=0) - member
    place = jnp.where(member == 1, before, -1).T.astype(F32)
    per_expert = jnp.sum(jnp.where(picked, route_weights[:, :, None], 0.0), axis=1).T
    high = lax.reduce_precision(per_expert, 8, 7)
    mid = lax.reduce_precision(per_expert - high, 8, 7)
    low = per_expert - high - mid
    flag = jnp.broadcast_to(chosen_set.astype(F32), (EXPERTS, seq_len))
    info = jnp.concatenate([place, high, mid, low, flag], axis=0).astype(BF)
    info_rows = 16
    info = info.reshape(-1, width)
    info = jnp.pad(info, ((0, info_rows - info.shape[0]), (0, 0)))
    cot_info = after(jnp.concatenate([cotangent, info], axis=0), *line2, *near_o)
    cot_line = lax.all_gather(cot_info, "shard")
    sent_w = jnp.concatenate([near1[:, : marks[2]], near2], axis=1)
    all_w = lax.all_gather(after(sent_w, normed_two), "rep")
    order = sorted(range(n_shard), key=lambda k: (k != 0, abs(2 * k - n_shard), k))
    rows_line = {0: normed_two}
    for k in order[1:]:
        rows_line[k] = line_send(normed_two, n_shard - k)
    params = (
        expert_gate,
        expert_upper,
        expert_lower,
        jnp.concatenate(
            [t.reshape(n_exp, width, PACK).transpose(0, 2, 1) for t in (gate_down, upper_down)],
            axis=1,
        ),
        gate_lift.reshape(n_exp, -1, PACK).transpose(0, 2, 1),
        upper_lift.reshape(n_exp, -1, PACK).transpose(0, 2, 1),
        lower_down.reshape(n_exp, -1, PACK).transpose(0, 2, 1),
        lower_lift.reshape(n_exp, width, PACK).transpose(0, 2, 1),
    )

    def read(facts):
        mine = lax.dynamic_slice_in_dim(facts.astype(F32), plane * n_exp, n_exp, 2)
        flags = (jnp.arange(SETS, dtype=F32) == mine[:, 4, 0, :1]).astype(F32)
        mask = jnp.tile(jnp.repeat(flags, RANK, axis=1), (1, 2))
        return mine[:, 0].astype(jnp.int32), mine[:, 1] + mine[:, 2] + mine[:, 3], mask

    fact_rows = 5 * EXPERTS * seq_len // width
    own_facts = read(info[:fact_rows].reshape(1, 5, EXPERTS, seq_len))
    line_facts = read(
        cot_line[:, seq_len : seq_len + fact_rows].reshape(n_shard, 5, EXPERTS, seq_len)
    )

    def chunk(k, prior):
        if k == 0:
            spot, share_of, mask = (f[0] for f in own_facts)
            cot, source = cotangent[None], jnp.zeros((1,), jnp.int32)
        else:
            source = (plane + k) % n_shard
            spot, share_of, mask = (
                lax.dynamic_index_in_dim(f, source, 0, keepdims=False) for f in line_facts
            )
            cot, source = cot_line, source.reshape(1).astype(jnp.int32)
        return expert_chunk(
            source,
            rows_line[k],
            cot,
            spot[:, None, :],
            share_of[:, None, :],
            mask[None],
            params,
            prior,
            F32 if k == 0 else BF,
        )

    results, prior = {}, None
    for k in order:
        results[k] = chunk(k, prior)
        prior = results[k][2:]
    back_parts = [line_send(results[k][1], k) for k in order[1:]]
    out_parts = [line_send(results[k][0], k) for k in order[1:]]
    expert_sums = [g.astype(BF) for g in prior]
    expert_sums = lax.psum(tuple(expert_sums), "rep")

    input_grad, attn_flat = attention_back(
        ids,
        (*masks, tokens, cotangent, after_attn, gain_one, gain_two, results[0][1])
        + (downs, lift_out, keep),
        back_parts,
        (mixed, r_own, r_out),
        qkv,
        near_o,
        far_o,
        all_w,
        sizes,
    )
    attn_flat = after(attn_flat, *out_parts)
    output = after_attn + results[0][0]
    for part in out_parts:
        output = output + part.astype(F32)
    output = output.astype(BF)

    def block_of(k):
        return lax.dynamic_index_in_dim(attn_flat, (plane + k) % n_shard, 0, keepdims=False)

    total = block_of(0).astype(F32)
    for k in range(1, n_shard):
        total = total + line_send(block_of(k), k).astype(F32)
    bits = n_rep.bit_length() - 1
    stages = [[1], [2, 4, 6]] if bits > 2 else [[1 << b] for b in range(bits)]
    stages = stages + [[1 << b] for b in range(3, bits)]
    for stage in stages:
        rounded = total.astype(BF)
        total = rounded.astype(F32)
        for swap in stage:
            total = total + rep_swap(rounded, swap).astype(F32)
    attn_flat = total

    def unflat(g):
        return g.T.reshape(cols, SETS, RANK)

    attn_outs = [unflat(attn_flat[a * PACK : (a + 1) * PACK]) for a in range(8)]

    parts = [g.astype(F32) for g in expert_sums]

    def restore(g):
        return g.transpose(0, 2, 1).reshape(n_exp, -1, SETS, RANK)

    expert_outs = [
        restore(parts[0][:, :PACK]),
        restore(parts[1]),
        restore(parts[0][:, PACK:]),
        restore(parts[2]),
        restore(parts[3]),
        restore(parts[4]),
    ]
    return (output, input_grad, *attn_outs, *expert_outs)


def solution(mesh):
    rows = P(("rep", "shard"), None)
    second = P(None, "shard")
    three = P("shard", None, None)
    four = P("shard", None, None, None)
    placed = (rows,) * 6 + (P(("rep", "shard")), P(), P()) + (second,) * 4
    placed = placed + (three,) * 11 + (four,) * 6
    return jax.shard_map(
        functools.partial(local, mesh.shape["rep"], mesh.shape["shard"]),
        mesh=mesh,
        in_specs=placed,
        out_specs=(rows, rows) + (three,) * 8 + (four,) * 6,
        check_vma=False,
    )
```

```python
import functools

import jax
import jax.numpy as jnp
from jax import lax
from jax.experimental import pallas as pl
from jax.experimental.pallas import tpu as pltpu
from jax.sharding import PartitionSpec as P

HEADS = 16
HEAD = 128
TOP = 8
EXPERTS = 16
RANK = 16
SETS = 2
MOST = 160
PACK = SETS * RANK

epsilon = 1e-06
adapter_scale = 2.0
masked_score = -1e30
score_scale = HEAD ** (-0.5)

BF = jnp.bfloat16
F32 = jnp.float32
VMEM = 56 * 1024 * 1024


def dot_nn(a, b):
    return jnp.dot(a, b, preferred_element_type=F32)


def dot_nt(a, b):
    return lax.dot_general(a, b, (((1,), (1,)), ((), ())), preferred_element_type=F32)


def dot_tn(a, b):
    return lax.dot_general(a, b, (((0,), (0,)), ((), ())), preferred_element_type=F32)


def rms_forward(values, gain_vec):
    inverse = lax.rsqrt(jnp.mean(values * values, axis=-1, keepdims=True) + epsilon)
    return values * inverse * gain_vec


def rms_backward(values, gain_vec, grad_norm):
    inverse = lax.rsqrt(jnp.mean(values * values, axis=-1, keepdims=True) + epsilon)
    weighted = grad_norm * gain_vec
    cubed = inverse * inverse * inverse
    return inverse * weighted - values * cubed * jnp.mean(values * weighted, axis=-1, keepdims=True)


def scores(q, k, allowed):
    s = dot_nt(q, k) * score_scale
    s = jnp.where(allowed, s, masked_score)
    e = jnp.exp(s - jnp.max(s, axis=-1, keepdims=True))
    return e / jnp.sum(e, axis=-1, keepdims=True)


def allowed_mask(seg_row, seg_col, pad_row):
    shape = (seg_col.shape[0], seg_row.shape[1])
    rows = lax.broadcasted_iota(jnp.int32, shape, 0)
    cols = lax.broadcasted_iota(jnp.int32, shape, 1)
    return (seg_col == seg_row) & ((pad_row == 1) | (rows == cols))


def project_kernel(sizes, ids, h, downs, *refs):
    team, n_line, rows, width = sizes
    near, far, refs = refs[0], refs[1], refs[2:]
    outs, (r_own, h_s, flag_s, w_s, r_s, lift_s, sems) = refs[:team], refs[team:]
    plane, chip, core = ids[0], ids[1], ids[2]
    half = width // 2
    lift_half = 3 * PACK // 2
    copies = []
    for j in range(team):
        source = ids[3] + (chip ^ j) * 2 + core
        copies.append(
            pltpu.make_async_copy(
                h.at[source, :rows], h_s.at[j * rows : (j + 1) * rows], sems.at[0, j]
            )
        )
        copies.append(
            pltpu.make_async_copy(h.at[source, rows:, :HEAD], flag_s.at[j], sems.at[1, j])
        )
    for copy in copies:
        copy.start()
    for k in range(n_line):
        at = pl.ds(pl.multiple_of((plane + k) % n_line * HEAD, HEAD), HEAD)
        for side, ref in ((core, near), (1 - core, far)):
            for a in range(3):
                start = a * half + (lift_half if a else 0)
                w_s[a, pl.ds(pl.multiple_of(side * half, half), half), at] = ref[
                    k, start : start + half, :
                ]
            lift_s[3, pl.ds(pl.multiple_of(side * lift_half, 16), lift_half), at] = ref[
                k, half : half + lift_half, :
            ]
    lifts = lift_s[3]
    band = lax.broadcasted_iota(jnp.int32, lifts.shape, 0) // PACK
    for a in range(3):
        lift_s[a] = jnp.where(band == a, lifts, jnp.zeros_like(lifts))
    for copy in copies:
        copy.wait()
    for j in range(team):
        at = slice(j * rows, (j + 1) * rows)
        keep = flag_s[j, :1, : 3 * PACK].astype(F32)
        r_s[at, :] = (dot_nt(h_s[at, :], downs[: 3 * PACK, :]) * keep).astype(BF)
    for a in range(3):
        r_own[a] = r_s[:rows, a * PACK : (a + 1) * PACK]
    span = n_line * HEAD
    tile = min(256, span)
    per = span // tile

    def step(i, carry):
        a = i // per
        at = pl.multiple_of((i % per) * tile, tile)
        y = dot_nn(h_s[...], w_s[a, :, pl.ds(at, tile)])
        y = y + adapter_scale * dot_nn(r_s[...], lift_s[a, :, pl.ds(at, tile)])
        y = y.astype(BF)
        for j in range(team):
            outs[j][:, pl.ds(pl.multiple_of(i * tile, tile), tile)] = y[j * rows : (j + 1) * rows]
        return carry

    lax.fori_loop(0, 3 * per, step, 0)


def project(ids, h, downs, near, far, sizes):
    team, n_line, rows, width = sizes
    span = n_line * HEAD
    full = pl.BlockSpec(memory_space=pltpu.VMEM)
    got = pl.pallas_call(
        functools.partial(project_kernel, sizes),
        in_specs=[pl.BlockSpec(memory_space=pltpu.SMEM), pl.BlockSpec(memory_space=pl.ANY)]
        + [full] * 3,
        out_specs=[full] * (team + 1),
        out_shape=[jax.ShapeDtypeStruct((rows, 3 * span), BF)] * team
        + [jax.ShapeDtypeStruct((3, rows, PACK), BF)],
        scratch_shapes=[
            pltpu.VMEM((team * rows, width), BF),
            pltpu.VMEM((team, 16, HEAD), BF),
            pltpu.VMEM((3, width, span), BF),
            pltpu.VMEM((team * rows, 3 * PACK), BF),
            pltpu.VMEM((4, 3 * PACK, span), BF),
            pltpu.SemaphoreType.DMA((2, team)),
        ],
        compiler_params=pltpu.CompilerParams(vmem_limit_bytes=VMEM),
        cost_estimate=pl.CostEstimate(
            flops=6 * team * rows * width * span, bytes_accessed=12 * width * span, transcendentals=0
        ),
    )(ids, h, downs, near, far)
    return got[:team], got[team]


def chip_columns(ref, chip, n_line, cols):
    parts = []
    for z in range(n_line):
        parts.append(ref[:, pl.ds(pl.multiple_of(z * cols + chip * HEAD, HEAD), HEAD)])
    return jnp.concatenate(parts, axis=1)


def mix_kernel(sizes, ids, seg_row, seg_col, pad_row, tokens, gain, d_out, l_out, keep, *refs):
    team, n_line, rows, width, cols = sizes
    qkv, refs = refs[:team], refs[team:]
    near, refs = refs[:team], refs[team:]
    far, refs = refs[:team], refs[team:]
    mixed, r_out, x1, h2, acc = refs
    chip, core = ids[1], ids[2]
    span = n_line * HEAD
    side = span // 2
    allowed = allowed_mask(seg_row[...], seg_col[...], pad_row[...])
    reduced = jnp.zeros((rows, PACK), F32)
    for j in range(team):
        for z in range(n_line):
            q, k, v = (
                qkv[j][:, a * span + z * HEAD : a * span + (z + 1) * HEAD] for a in range(3)
            )
            p = scores(q, k, allowed)
            mixed[:, j * span + z * HEAD : j * span + (z + 1) * HEAD] = dot_nn(
                p.astype(BF), v
            ).astype(BF)
        o = mixed[:, j * span : (j + 1) * span]
        reduced = reduced + dot_nt(o, chip_columns(d_out, chip ^ j, n_line, cols))
        mine = mixed[:, pl.ds(pl.multiple_of(j * span + core * side, HEAD), side)]
        other = mixed[:, pl.ds(pl.multiple_of(j * span + (1 - core) * side, HEAD), side)]
        part = dot_nn(mine, near[j][...]) + dot_nn(other, far[j][...])
        if j == 0:
            acc[...] = part
        else:
            acc[...] += part
    low = (reduced * keep[...]).astype(BF)
    r_out[...] = low
    total = tokens[...].astype(F32) + (acc[...] + adapter_scale * dot_nn(low, l_out[...]))
    x1[...] = total
    h2[...] = rms_forward(total, gain[...]).astype(BF)


def mix(ids, masks, tokens, gain, d_out, l_out, keep, qkv, near, far, sizes):
    team, n_line, rows, width, cols = sizes
    full = pl.BlockSpec(memory_space=pltpu.VMEM)
    return pl.pallas_call(
        functools.partial(mix_kernel, sizes),
        in_specs=[pl.BlockSpec(memory_space=pltpu.SMEM)] + [full] * (8 + 3 * team),
        out_specs=[full] * 4,
        out_shape=[
            jax.ShapeDtypeStruct((rows, width), BF),
            jax.ShapeDtypeStruct((rows, PACK), BF),
            jax.ShapeDtypeStruct((rows, width), F32),
            jax.ShapeDtypeStruct((rows, width), BF),
        ],
        scratch_shapes=[pltpu.VMEM((rows, width), F32)],
        compiler_params=pltpu.CompilerParams(vmem_limit_bytes=VMEM),
        cost_estimate=pl.CostEstimate(
            flops=2 * rows * width * width + 4 * rows * rows * width,
            bytes_accessed=2 * width * width + 12 * rows * width,
            transcendentals=rows * rows * HEADS,
        ),
    )(ids, *masks, tokens, gain, d_out, l_out, keep, *qkv, *near, *far)


def back_kernel(sizes, n_parts, ids, *refs):
    team, n_line, rows, width, cols = sizes
    (seg_row, seg_col, pad_row, tokens, cot, x1, gain1, gain2, own, downs, l_out, keep) = refs[:12]
    refs = refs[12:]
    parts, refs = refs[:n_parts], refs[n_parts:]
    mixed, r_own, r_out = refs[:3]
    refs = refs[3:]
    qkv, refs = refs[:team], refs[team:]
    near_o, refs = refs[:team], refs[team:]
    far_o, refs = refs[:team], refs[team:]
    weights, in_grad, grads, near_s, far_s, sems, dx1_s, da_s, do_s, do_b, dp_s, acc, h1_s, dr, lift_s = refs
    chip, core = ids[1], ids[2]
    span = n_line * HEAD
    side = span // 2
    half = width // 2
    lift_gap = 3 * PACK // 2
    lift_end = half + lift_gap
    slots = near_s.shape[0]

    def fetch(j):
        copies = []
        for side_at, buf in ((core, near_s), (1 - core, far_s)):
            source = ids[3] + (chip ^ j) * 2 + side_at
            number = 0 if buf is near_s else 1
            for z in range(n_line):
                at = pl.multiple_of((ids[0] + z) % n_line * HEAD, HEAD)
                copies.append(
                    pltpu.make_async_copy(
                        weights.at[source, z],
                        buf.at[j % slots, :, pl.ds(at, HEAD)],
                        sems.at[j % slots, number, z],
                    )
                )
        return copies

    for copy in fetch(0):
        copy.start()
    mask = keep[...]
    dh2 = own[...]
    for part in parts:
        dh2 = dh2 + part[...].astype(F32)
    dx1 = cot[...].astype(F32) + rms_backward(x1[...], gain2[...], dh2)
    dx1_s[...] = dx1
    da_s[...] = dx1.astype(BF)
    h1_s[...] = rms_forward(tokens[...].astype(F32), gain1[...]).astype(BF)
    da = da_s[...]
    d_low = (adapter_scale * dot_nt(da, l_out[...]) * mask).astype(BF)

    def put_all(row, block):
        for z in range(n_line):
            part = block[:, z * cols : (z + 1) * cols]
            grads[z, row : row + RANK, :] = (part[:RANK] + part[RANK:]).astype(BF)

    put_all(7 * RANK, adapter_scale * dot_tn(r_out[...], da))
    allowed = allowed_mask(seg_row[...], seg_col[...], pad_row[...])
    dr[...] = jnp.zeros_like(dr)
    here = pl.multiple_of(core * half, half)
    there = pl.multiple_of((1 - core) * half, half)
    acc[...] = jnp.zeros_like(acc)
    for j in range(team):
        ahead = j + slots - 1
        if 0 < ahead < team:
            for copy in fetch(ahead):
                copy.start()
        spot = chip ^ j

        def put(row, block):
            for z in range(n_line):
                at = pl.multiple_of(spot * HEAD, HEAD)
                part = block[:, z * HEAD : (z + 1) * HEAD]
                part = part[:RANK] + part[RANK:]
                grads[z, pl.ds(row, RANK), pl.ds(at, HEAD)] = part.astype(BF)

        do_s[:, pl.ds(pl.multiple_of(core * side, HEAD), side)] = dot_nt(da, near_o[j][...])
        do_s[:, pl.ds(pl.multiple_of((1 - core) * side, HEAD), side)] = dot_nt(da, far_o[j][...])
        do = do_s[...] + dot_nn(
            d_low, chip_columns(downs.at[3 * PACK :, :], spot, n_line, cols)
        )
        do = do.astype(BF)
        put(3 * RANK, dot_tn(d_low, mixed[:, j * span : (j + 1) * span]))
        do_b[...] = do

        def head(z, carry):
            at = pl.multiple_of(z * HEAD, HEAD)
            q, k, v = (
                qkv[j][:, pl.ds(pl.multiple_of(a * span + at, HEAD), HEAD)] for a in range(3)
            )
            p = scores(q, k, allowed)
            do_h = do_b[:, pl.ds(at, HEAD)]
            dp = dot_nt(do_h, v)
            delta = jnp.sum(dp * p, axis=-1, keepdims=True)
            ds = (p * (dp - delta)).astype(BF)
            heads = (
                dot_nn(ds, k) * score_scale,
                dot_tn(ds, q) * score_scale,
                dot_tn(p.astype(BF), do_h),
            )
            for a in range(3):
                dp_s[:, pl.ds(pl.multiple_of(a * span + at, HEAD), HEAD)] = heads[a].astype(BF)
            return carry

        lax.fori_loop(0, n_line, head, 0, unroll=2)
        for copy in fetch(j):
            copy.wait()
        slot = j % slots
        packs = jnp.where(
            core == 0,
            jnp.concatenate([near_s[slot, half:lift_end, :], far_s[slot, half:lift_end, :]]),
            jnp.concatenate([far_s[slot, half:lift_end, :], near_s[slot, half:lift_end, :]]),
        )
        for a in range(3):
            lift_s[a] = packs[a * PACK : (a + 1) * PACK]

        def grad(a, carry):
            g = dp_s[:, pl.ds(pl.multiple_of(a * span, HEAD), span)]
            lift = lift_s[a]
            dr[a] += dot_nt(g, lift)
            put(
                pl.multiple_of((4 + a) * RANK, RANK), adapter_scale * dot_tn(r_own[a], g)
            )
            rows_a = pl.ds(pl.multiple_of(a * half + lift_gap * jnp.minimum(a, 1), 16), half)
            acc[:, pl.ds(here, half)] += dot_nt(g, near_s[slot, rows_a, :])
            acc[:, pl.ds(there, half)] += dot_nt(g, far_s[slot, rows_a, :])
            return carry

        lax.fori_loop(0, 3, grad, 0)
    h1 = h1_s[...]
    for a in range(3):
        low = (adapter_scale * dr[a] * mask).astype(BF)
        put_all(a * RANK, dot_tn(low, h1))
        acc[...] += dot_nn(low, downs[a * PACK : (a + 1) * PACK, :])
    total = dx1_s[...] + rms_backward(tokens[...].astype(F32), gain1[...], acc[...])
    in_grad[...] = total.astype(BF)


def attention_back(ids, small, parts, kept, qkv, near_o, far_o, weights, sizes):
    team, n_line, rows, width, cols = sizes
    span = n_line * HEAD
    full = pl.BlockSpec(memory_space=pltpu.VMEM)
    count = len(small) + len(parts) + len(kept) + 3 * team
    slots = 2 if span <= 512 else 1
    return pl.pallas_call(
        functools.partial(back_kernel, sizes, len(parts)),
        in_specs=[pl.BlockSpec(memory_space=pltpu.SMEM)]
        + [full] * count
        + [pl.BlockSpec(memory_space=pl.ANY)],
        out_specs=[full] * 2,
        out_shape=[
            jax.ShapeDtypeStruct((rows, width), BF),
            jax.ShapeDtypeStruct((n_line, 8 * RANK, cols), BF),
        ],
        scratch_shapes=[
            pltpu.VMEM((slots, weights.shape[2], span), BF),
            pltpu.VMEM((slots, weights.shape[2], span), BF),
            pltpu.SemaphoreType.DMA((slots, 2, n_line)),
            pltpu.VMEM((rows, width), F32),
            pltpu.VMEM((rows, width), BF),
            pltpu.VMEM((rows, span), F32),
            pltpu.VMEM((rows, span), BF),
            pltpu.VMEM((rows, 3 * span), BF),
            pltpu.VMEM((rows, width), F32),
            pltpu.VMEM((rows, width), BF),
            pltpu.VMEM((3, rows, PACK), F32),
            pltpu.VMEM((3, PACK, span), BF),
        ],
        compiler_params=pltpu.CompilerParams(vmem_limit_bytes=VMEM),
        cost_estimate=pl.CostEstimate(
            flops=8 * rows * width * width + 10 * rows * rows * width,
            bytes_accessed=8 * width * width + 20 * rows * width,
            transcendentals=rows * rows * HEADS,
        ),
    )(ids, *small, *parts, *kept, *qkv, *near_o, *far_o, weights)


def expert_kernel(
    n_exp,
    has_sum,
    tile,
    source,
    h2,
    place,
    weight,
    mask,
    dy_in,
    dm_in,
    drl_in,
    w_gate,
    w_up,
    w_low,
    d_gu,
    l_gate,
    l_up,
    d_low,
    l_low,
    *refs,
):
    prior = None
    if has_sum:
        prior, refs = refs[0], refs[1:]
    (out, dh2, grads) = refs[:3]
    (x_s, hid_s, dg_s, du_s, sel, y_all, dx_all) = refs[3:]
    ff = w_gate.shape[2]

    def emit(row, value, column=0):
        at = (0, slice(row, row + value.shape[0]), slice(column, column + value.shape[1]))
        if has_sum:
            value = value + prior[at]
        grads[at] = value.astype(grads.dtype)

    e = pl.program_id(0)
    keep = mask[...]
    keep_one = keep[:, :PACK]
    base = pl.multiple_of(e * MOST, MOST)
    slots = lax.broadcasted_iota(jnp.int32, (MOST, place.shape[2]), 0)
    hit = slots == place[0]
    pick = jnp.where(hit, 1.0, 0.0).astype(BF)
    sel[pl.ds(base, MOST), :] = pick
    sw = jnp.sum(jnp.where(hit, weight[0], 0.0), axis=1, keepdims=True)
    x_s[...] = dot_nn(pick, h2[...]).astype(BF)
    x = x_s[...]
    dy = dy_in[0, 0]
    r_gu = (dot_nt(x, d_gu[0]) * keep).astype(BF)
    r_g, r_u = r_gu[:, :PACK], r_gu[:, PACK:]
    dr_low = drl_in[0, 0]
    for start in range(0, w_gate.shape[2], tile):
        at = slice(start, start + tile)
        gate = dot_nn(x, w_gate[0, :, at]) + adapter_scale * dot_nn(r_g, l_gate[0, :, at])
        up = dot_nn(x, w_up[0, :, at]) + adapter_scale * dot_nn(r_u, l_up[0, :, at])
        d_hidden = dm_in[0, 0, :, at].astype(F32)
        sig = 1.0 / (1.0 + jnp.exp(-gate))
        act = gate * sig
        hid_s[:, at] = (act * up).astype(BF)
        dg_s[:, at] = (d_hidden * up * sig * (1.0 + gate * (1.0 - sig))).astype(BF)
        du_s[:, at] = (d_hidden * act).astype(BF)
    hidden, d_gate, d_up = hid_s[...], dg_s[...], du_s[...]
    r_low = (dot_nt(hidden, d_low[0]) * keep_one).astype(BF)
    y = dot_nn(hidden, w_low[0]) + adapter_scale * dot_nn(r_low, l_low[0])
    y_all[pl.ds(base, MOST), :] = (y * sw).astype(BF)
    dr = jnp.concatenate([dot_nt(d_gate, l_gate[0]), dot_nt(d_up, l_up[0])], axis=1)
    dr = (adapter_scale * dr * keep).astype(BF)
    dx = dot_nt(d_gate, w_gate[0]) + dot_nt(d_up, w_up[0]) + dot_nn(dr, d_gu[0])
    dx_all[pl.ds(base, MOST), :] = dx.astype(BF)
    emit(0, dot_tn(dr, x))
    emit(2 * PACK, adapter_scale * dot_tn(r_g, d_gate))
    emit(2 * PACK, adapter_scale * dot_tn(r_u, d_up), ff)
    emit(3 * PACK, adapter_scale * dot_tn(r_low, dy))
    g_low = dot_tn(dr_low, hidden)
    emit(4 * PACK, g_low[:RANK])
    emit(4 * PACK, g_low[RANK:], ff)

    @pl.when(e == n_exp - 1)
    def _():
        out[...] = dot_tn(sel[...], y_all[...]).astype(out.dtype)
        dh2[...] = dot_tn(sel[...], dx_all[...]).astype(dh2.dtype)


def grad_kernel(n_line, tile, cot, place, weight, mask, w_low, d_low, l_low, dy, dm, drl, dy_s):
    slots = lax.broadcasted_iota(jnp.int32, (MOST, place.shape[3]), 0)
    for k in range(n_line):
        hit = slots == place[k, 0]
        pick = jnp.where(hit, 1.0, 0.0).astype(BF)
        sw = jnp.sum(jnp.where(hit, weight[k, 0], 0.0), axis=1, keepdims=True)
        block = (dot_nn(pick, cot[k]) * sw).astype(BF)
        dy_s[k * MOST : (k + 1) * MOST, :] = block
        dy[k, 0] = block
    full = dy_s[...]
    dr = adapter_scale * dot_nt(full, l_low[0])
    dr = jnp.concatenate(
        [dr[k * MOST : (k + 1) * MOST] * mask[k, :, :PACK] for k in range(n_line)], axis=0
    ).astype(BF)
    for k in range(n_line):
        drl[k, 0] = dr[k * MOST : (k + 1) * MOST]
    for start in range(0, w_low.shape[1], tile):
        at = slice(start, start + tile)
        block = dot_nt(full, w_low[0, at, :]) + dot_nn(dr, d_low[0, :, at])
        block = block.astype(BF)
        for k in range(n_line):
            dm[k, 0, :, at] = block[k * MOST : (k + 1) * MOST]


def grad_rows(cot, place, weight, mask, w_low, d_low, l_low):
    n_line, rows, width = cot.shape
    n_exp, ff = w_low.shape[:2]
    per_e = lambda e: (e, 0, 0)
    all_e = lambda e: (0, e, 0, 0)
    return pl.pallas_call(
        functools.partial(grad_kernel, n_line, 256),
        grid=(n_exp,),
        in_specs=[
            pl.BlockSpec((n_line, rows, width), lambda e: (0, 0, 0)),
            pl.BlockSpec((n_line, 1, 1, rows), all_e),
            pl.BlockSpec((n_line, 1, 1, rows), all_e),
            pl.BlockSpec((n_line, 1, 2 * PACK), lambda e: (0, 0, 0)),
            pl.BlockSpec((1, ff, width), per_e),
            pl.BlockSpec((1, PACK, ff), per_e),
            pl.BlockSpec((1, PACK, width), per_e),
        ],
        out_specs=[
            pl.BlockSpec((n_line, 1, MOST, width), all_e),
            pl.BlockSpec((n_line, 1, MOST, ff), all_e),
            pl.BlockSpec((n_line, 1, MOST, PACK), all_e),
        ],
        out_shape=[
            jax.ShapeDtypeStruct((n_line, n_exp, MOST, width), BF),
            jax.ShapeDtypeStruct((n_line, n_exp, MOST, ff), BF),
            jax.ShapeDtypeStruct((n_line, n_exp, MOST, PACK), BF),
        ],
        scratch_shapes=[pltpu.VMEM((n_line * MOST, width), BF)],
        compiler_params=pltpu.CompilerParams(
            vmem_limit_bytes=VMEM, dimension_semantics=("arbitrary",)
        ),
        cost_estimate=pl.CostEstimate(
            flops=3 * n_line * n_exp * MOST * width * ff,
            bytes_accessed=2 * n_exp * width * ff,
            transcendentals=0,
        ),
    )(cot, place, weight, mask, w_low, d_low, l_low)


def expert_chunk(source, h2, ready, place, weight, mask, params, prior, out_type, grad_type=F32):
    w_gate, w_up, w_low, d_gu, l_gate, l_up, d_low, l_low = params
    n_exp, width, ff = w_gate.shape
    rows = h2.shape[0]
    whole = lambda e, s: (0, 0)
    per_e = lambda e, s: (e, 0, 0)
    grad_specs = [pl.BlockSpec((1, 4 * PACK + RANK, width), per_e)]
    return pl.pallas_call(
        functools.partial(expert_kernel, n_exp, prior is not None, 256),
        grid_spec=pltpu.PrefetchScalarGridSpec(
            num_scalar_prefetch=1,
            grid=(n_exp,),
            in_specs=[
                pl.BlockSpec((rows, width), whole),
                pl.BlockSpec((1, 1, rows), per_e),
                pl.BlockSpec((1, 1, rows), per_e),
                pl.BlockSpec((1, 2 * PACK), whole),
                pl.BlockSpec((1, 1, MOST, width), lambda e, s: (s[0], e, 0, 0)),
                pl.BlockSpec((1, 1, MOST, ff), lambda e, s: (s[0], e, 0, 0)),
                pl.BlockSpec((1, 1, MOST, PACK), lambda e, s: (s[0], e, 0, 0)),
                pl.BlockSpec((1, width, ff), per_e),
                pl.BlockSpec((1, width, ff), per_e),
                pl.BlockSpec((1, ff, width), per_e),
                pl.BlockSpec((1, 2 * PACK, width), per_e),
                pl.BlockSpec((1, PACK, ff), per_e),
                pl.BlockSpec((1, PACK, ff), per_e),
                pl.BlockSpec((1, PACK, ff), per_e),
                pl.BlockSpec((1, PACK, width), per_e),
            ]
            + (grad_specs if prior is not None else []),
            out_specs=[
                pl.BlockSpec((rows, width), whole),
                pl.BlockSpec((rows, width), whole),
            ]
            + grad_specs,
            scratch_shapes=[
                pltpu.VMEM((MOST, width), BF),
                pltpu.VMEM((MOST, ff), BF),
                pltpu.VMEM((MOST, ff), BF),
                pltpu.VMEM((MOST, ff), BF),
                pltpu.VMEM((n_exp * MOST, rows), BF),
                pltpu.VMEM((n_exp * MOST, width), BF),
                pltpu.VMEM((n_exp * MOST, width), BF),
            ],
        ),
        out_shape=[
            jax.ShapeDtypeStruct((rows, width), out_type),
            jax.ShapeDtypeStruct((rows, width), out_type),
        ]
        + [jax.ShapeDtypeStruct((n_exp, 4 * PACK + RANK, width), grad_type)],
        compiler_params=pltpu.CompilerParams(
            vmem_limit_bytes=VMEM, dimension_semantics=("arbitrary",)
        ),
        cost_estimate=pl.CostEstimate(
            flops=16 * n_exp * MOST * width * ff,
            bytes_accessed=6 * n_exp * width * ff,
            transcendentals=n_exp * MOST * ff,
        ),
    )(
        source,
        h2,
        place,
        weight,
        mask,
        *ready,
        w_gate,
        w_up,
        w_low,
        d_gu,
        l_gate,
        l_up,
        d_low,
        l_low,
        *(prior or ()),
    )


def local(
    n_rep,
    n_shard,
    tokens,
    cotangent,
    segments,
    padding,
    routes,
    route_weights,
    adapter_set,
    norm_one,
    norm_two,
    query_weight,
    key_weight,
    value_weight,
    output_weight,
    query_down,
    key_down,
    value_down,
    output_down,
    query_lift,
    key_lift,
    value_lift,
    output_lift,
    expert_gate,
    expert_upper,
    expert_lower,
    gate_down,
    gate_lift,
    upper_down,
    upper_lift,
    lower_down,
    lower_lift,
):
    seq_len, width = tokens.shape
    n_exp, _, ff = expert_gate.shape
    cols = query_weight.shape[1]
    team = min(cols // HEAD, n_rep // 2)
    tiles = cols // HEAD
    half = width // 2
    plane = lax.axis_index("shard")
    rep = lax.axis_index("rep")
    core = rep % 2
    chip = (rep // 2) % team
    ids = jnp.stack([plane, chip, core, rep - rep % (2 * team)]).astype(jnp.int32)

    def rep_swap(x, bits):
        return lax.ppermute(x, "rep", [(a, a ^ bits) for a in range(n_rep)])

    def line_step(up, down):
        return (
            lax.ppermute(up, "shard", [(a, a - 1) for a in range(1, n_shard)]),
            lax.ppermute(down, "shard", [(a, a + 1) for a in range(n_shard - 1)]),
        )

    def line_steps(x):
        steps = [(x, x)]
        for _ in range(1, n_shard):
            steps.append(line_step(*steps[-1]))
        return steps

    def line_join(steps):
        joined = [steps[0][0]]
        for k in range(1, n_shard):
            joined.append(steps[k][0] + steps[n_shard - k][1])
        return joined

    def line_send(x, k):
        return lax.ppermute(x, "shard", [(a, (a + k) % n_shard) for a in range(n_shard)])

    def in_order(parts):
        buf = jnp.zeros((n_shard,) + parts[0].shape, parts[0].dtype)
        for k, part in enumerate(parts):
            buf = lax.dynamic_update_index_in_dim(buf, part, (plane + k) % n_shard, 0)
        return buf

    def chip_gather(x):
        return [x] + [rep_swap(x, j << 1) for j in range(1, team)]

    def after(x, *others):
        return lax.optimization_barrier((x,) + others)[0]

    chosen_set = adapter_set[0]
    set_flags = (jnp.arange(SETS, dtype=jnp.int32) == chosen_set).astype(F32)
    keep = jnp.repeat(set_flags, RANK)[None]
    masks = (segments, segments.reshape(seq_len, 1), padding)
    gain_one, gain_two = norm_one[None], norm_two[None]
    normed_one = rms_forward(tokens.astype(F32), gain_one).astype(BF)
    flag_rows = jnp.pad(jnp.tile(keep, (16, 3)), ((0, 0), (0, width - 3 * PACK))).astype(BF)
    all_h = lax.all_gather(jnp.concatenate([normed_one, flag_rows], axis=0), "rep")

    expert_ids = jnp.arange(EXPERTS, dtype=jnp.int32)
    picked = routes[:, :, None] == expert_ids[None, None, :]
    member = jnp.sum(picked.astype(jnp.int32), axis=1)
    before = jnp.cumsum(member, axis=0) - member
    place = jnp.where(member == 1, before, -1).T.astype(F32)
    per_expert = jnp.sum(jnp.where(picked, route_weights[:, :, None], 0.0), axis=1).T
    high = lax.reduce_precision(per_expert, 8, 7)
    mid = lax.reduce_precision(per_expert - high, 8, 7)
    low = per_expert - high - mid
    flag = jnp.broadcast_to(chosen_set.astype(F32), (EXPERTS, seq_len))
    info = jnp.concatenate([place, high, mid, low, flag], axis=0).astype(BF)
    fact_rows = info.size // HEAD

    def flat(table):
        return table.reshape(table.shape[0], PACK).T

    def pieces(x):
        return x.reshape(x.shape[0], tiles, HEAD).transpose(1, 0, 2).reshape(-1, HEAD)

    def whole_rows(x, height):
        x = x.reshape(n_shard, tiles, height, HEAD)
        return x.transpose(2, 0, 1, 3).reshape(height, width)

    def both(a, b, axis=0):
        return jnp.where(
            core == 0, jnp.concatenate([a, b], axis=axis), jnp.concatenate([b, a], axis=axis)
        )

    def slice_of(weight):
        return lax.dynamic_slice(weight, (core * half, chip * HEAD), (half, HEAD))

    def core_rows(table, height):
        return lax.dynamic_slice(table, (core * height, 0), (height, table.shape[1]))

    lift_rows = 3 * PACK // 2
    down_rows = 4 * PACK // 2
    last_rows = PACK // 2
    lift_pack = jnp.concatenate([flat(t) for t in (query_lift, key_lift, value_lift)], axis=0)
    down_pack = jnp.concatenate(
        [flat(t) for t in (query_down, key_down, value_down, output_down)], axis=0
    )
    out_rows = output_weight.reshape(2, n_shard // 2, tiles, HEAD, cols)
    out_own = lax.dynamic_slice(
        out_rows, (core, 0, chip, 0, 0), (1, n_shard // 2, 1, HEAD, cols)
    ).reshape(n_shard // 2 * HEAD, cols)
    first = [
        pieces(core_rows(down_pack, down_rows)),
        pieces(core_rows(flat(output_lift), last_rows)),
        info.reshape(fact_rows, HEAD),
        pieces(out_own),
    ]
    marks = [0]
    for piece in first:
        marks.append(marks[-1] + piece.shape[0])
    second = [
        slice_of(query_weight),
        lax.dynamic_slice(lift_pack, (core * lift_rows, chip * HEAD), (lift_rows, HEAD)),
        slice_of(key_weight),
        slice_of(value_weight),
    ]
    steps1 = line_steps(jnp.concatenate(first, axis=0))
    line1 = line_join(steps1)
    near1 = in_order(line1)
    out_block = whole_rows(near1[:, marks[3] :], n_shard // 2 * HEAD)
    steps2 = [(after(jnp.concatenate(second, axis=0), *steps1[-2]),) * 2]
    for number in range(1, n_shard):
        last = steps2[-1]
        steps2.append(line_step(*(after(last, out_block) if number == 2 else last)))
    line2 = jnp.stack(line_join(steps2))
    far1 = rep_swap(near1[:, : marks[2]], 1)
    downs = both(*(whole_rows(g[:, : marks[1]], down_rows) for g in (near1, far1)))
    lift_out = both(*(whole_rows(g[:, marks[1] : marks[2]], last_rows) for g in (near1, far1)))
    near_o = chip_gather(out_block)
    far2 = rep_swap(line2, 1)

    params = (
        expert_gate,
        expert_upper,
        expert_lower,
        jnp.concatenate(
            [t.reshape(n_exp, width, PACK).transpose(0, 2, 1) for t in (gate_down, upper_down)],
            axis=1,
        ),
        gate_lift.reshape(n_exp, -1, PACK).transpose(0, 2, 1),
        upper_lift.reshape(n_exp, -1, PACK).transpose(0, 2, 1),
        lower_down.reshape(n_exp, -1, PACK).transpose(0, 2, 1),
        lower_lift.reshape(n_exp, width, PACK).transpose(0, 2, 1),
    )

    def read(facts):
        mine = lax.dynamic_slice_in_dim(facts.astype(F32), plane * n_exp, n_exp, 2)
        flags = (jnp.arange(SETS, dtype=F32) == mine[:, 4, 0, :1]).astype(F32)
        mask = jnp.tile(jnp.repeat(flags, RANK, axis=1), (1, 2))
        return mine[:, 0].astype(jnp.int32), mine[:, 1] + mine[:, 2] + mine[:, 3], mask

    line_facts = read(near1[:, marks[2] : marks[3]].reshape(n_shard, 5, EXPERTS, seq_len))

    sizes = (team, n_shard, seq_len, width)
    made, r_own = project(ids, all_h, downs, line2, far2, sizes)
    made, near_o = lax.optimization_barrier((tuple(made), tuple(near_o)))
    far_o = [rep_swap(b, 1) for b in near_o]
    qkv = [made[0]] + [rep_swap(made[j], j << 1) for j in range(1, team)]
    sizes = sizes + (cols,)
    mixed, r_out, after_attn, normed_two = mix(
        ids, masks, tokens, gain_two, downs[3 * PACK :], lift_out, keep, qkv, near_o, far_o, sizes
    )

    table = [
        sorted((b for b in range(n_shard) if b != a), key=lambda b, a=a: (abs(a - b), a - b))
        for a in range(n_shard)
    ]

    def slot_facts(number):
        source = plane.astype(jnp.int32)
        if number is not None:
            source = sum(jnp.where(plane == a, t[number], 0) for a, t in enumerate(table))
            source = source.astype(jnp.int32)
        spot, share_of, mask = (
            lax.dynamic_index_in_dim(f, source, 0, keepdims=False) for f in line_facts
        )
        return source.reshape(1), spot[:, None], share_of[:, None], mask[None]

    facts_of = {number: slot_facts(number) for number in (*range(n_shard - 1), None)}
    early = [f for facts in facts_of.values() for f in facts]
    cot_line = lax.all_gather(
        after(cotangent, line2, all_h, *params, *line_facts, *early), "shard"
    )
    all_w = lax.all_gather(after(line2, normed_two), "rep")
    row_steps = [(normed_two, normed_two)]
    row_steps.append(line_step(*row_steps[0]))

    def choose(options):
        groups = []
        for a, array in options.items():
            for group in groups:
                if group[0] is array:
                    group[1].append(a)
                    break
            else:
                groups.append((array, [a]))
        value = groups[0][0]
        for array, planes in groups[1:]:
            here = plane == planes[0]
            for a in planes[1:]:
                here = here | (plane == a)
            value = jnp.where(here, array, value)
        return value

    def slot_rows(number):
        options = {}
        for a in range(n_shard):
            far = table[a][number] - a
            options[a] = row_steps[far][0] if far > 0 else row_steps[-far][1]
        return choose(options)

    def send_back(x, number):
        rounds = []
        for a in range(n_shard):
            pair = (a, table[a][number])
            for pairs in rounds:
                if all(pair[1] != q[1] for q in pairs):
                    pairs.append(pair)
                    break
            else:
                rounds.append([pair])
        return [lax.ppermute(x, "shard", pairs) for pairs in rounds]

    spots, shares, set_masks = line_facts
    ready = grad_rows(
        cot_line,
        spots[:, :, None],
        shares[:, :, None],
        set_masks[:, None],
        after(expert_lower, normed_two),
        params[6],
        params[7],
    )

    row_steps[1] = after(row_steps[1], ready[1])
    row_steps.append(line_step(*row_steps[1]))

    def chunk(number, prior, waits):
        rows = normed_two if number is None else slot_rows(number)
        source, spot, share_of, mask = facts_of[number]
        if waits:
            rows = after(rows, *waits)
        return expert_chunk(
            source,
            rows,
            ready,
            spot,
            share_of,
            mask,
            params,
            prior,
            F32 if number is None else BF,
            BF if number is None else F32,
        )

    results, prior, parts = [], None, []
    for number in range(n_shard - 1):
        waits = parts[-2] if number > 1 else ()
        results.append(chunk(number, prior, waits))
        prior = results[-1][2:]
        parts.append(send_back(results[-1][1], number))
        done = number + 2
        if done < n_shard:
            row_steps[done] = after(row_steps[done], results[-1][1])
            if done + 1 < n_shard:
                row_steps.append(line_step(*row_steps[done]))
    own = chunk(None, prior, parts[-2] if n_shard > 2 else ())
    back_parts = [part for pair in parts for part in pair]
    prior, dh2 = own[2:], own[1]
    if len(back_parts) > 6:
        dh2 = dh2 + sum(part.astype(F32) for part in back_parts)
        back_parts = []

    def partial_for(far):
        options = {}
        for a in range(n_shard):
            if 0 <= a + far < n_shard:
                options[a] = results[table[a].index(a + far)][0]
        return choose(options).astype(F32)

    out_steps, up, down = [], None, None
    for far in range(n_shard - 1, 0, -1):
        right, left = partial_for(far), partial_for(-far)
        if up is not None:
            if far == n_shard - 2:
                up, down = after((up, down), own[1])
            right, left = right + up.astype(F32), left + down.astype(F32)
        up = lax.ppermute(
            right.astype(BF), "shard", [(a, a + 1) for a in range(n_shard - far)]
        )
        down = lax.ppermute(
            left.astype(BF), "shard", [(a, a - 1) for a in range(far, n_shard)]
        )
        out_steps.append((up, down))
    pack_shape = prior[0].shape
    split = prior[0].reshape(2, -1, width)
    taken = rep_swap(lax.dynamic_index_in_dim(split, 1 - core, 0, keepdims=False), 1)

    input_grad, attn_flat = attention_back(
        ids,
        (*masks, after(tokens, *out_steps[0]), cotangent, after_attn, gain_one, gain_two, dh2)
        + (downs, lift_out, keep),
        back_parts,
        (mixed, r_own, r_out),
        qkv,
        near_o,
        far_o,
        all_w,
        sizes,
    )
    taken = after(taken, attn_flat)
    mine = lax.dynamic_index_in_dim(split, core, 0, keepdims=False).astype(F32)
    split = (mine + taken.astype(F32)).astype(BF).reshape(team, -1, width)
    chip_total = lax.dynamic_index_in_dim(split, chip, 0, keepdims=False).astype(F32)
    expert_parts = [
        rep_swap(lax.dynamic_index_in_dim(split, chip ^ j, 0, keepdims=False), j << 1)
        for j in range(1, team)
    ]
    for part in expert_parts:
        chip_total = chip_total + part.astype(F32)
    for b in range(team.bit_length(), n_rep.bit_length() - 1):
        rounded = chip_total.astype(BF)
        chip_total = rounded.astype(F32) + rep_swap(rounded, 1 << b).astype(F32)
    rounded = chip_total.astype(BF)
    half_total = jnp.zeros((team,) + rounded.shape, BF)
    for j, part in enumerate(chip_gather(rounded)):
        half_total = lax.dynamic_update_index_in_dim(half_total, part, chip ^ j, 0)
    expert_sums = both(half_total[None], rep_swap(half_total, 1)[None]).reshape(pack_shape)
    if n_shard > 2:
        attn_flat = after(attn_flat, *out_steps[-2])
    output = after_attn + own[0] + up.astype(F32) + down.astype(F32)
    output = output.astype(BF)

    def block_of(k):
        return lax.dynamic_index_in_dim(attn_flat, (plane + k) % n_shard, 0, keepdims=False)

    def placed(part, k):
        own_set = lax.dynamic_index_in_dim(set_masks[:, RANK], (plane - k) % n_shard, 0)
        hit = own_set == jnp.arange(SETS, dtype=F32)
        return jnp.where(hit[:, None, None], part.astype(F32)[None], 0.0)

    total = placed(block_of(0), 0)
    for k in range(1, n_shard):
        total = total + placed(line_send(block_of(k), k), k)
    rounded = total.astype(BF)
    total = rounded.astype(F32) + rep_swap(rounded, 1).astype(F32)
    total = lax.dynamic_index_in_dim(total, core, 0, keepdims=False)
    bits = n_rep.bit_length() - 1
    stages = [[2, 4, 6]] if bits > 2 else [[1 << b] for b in range(1, bits)]
    stages = stages + [[1 << b] for b in range(3, bits)]
    for stage in stages:
        rounded = total.astype(BF)
        total = rounded.astype(F32)
        for swap in stage:
            total = total + rep_swap(rounded, swap).astype(F32)
    rounded = total.astype(BF)
    attn_flat = both(rounded[None], rep_swap(rounded, 1)[None]).astype(F32)

    def unflat(g):
        return g.transpose(2, 0, 1)

    attn_outs = [unflat(attn_flat[:, a * RANK : (a + 1) * RANK]) for a in range(8)]

    def restore(row, height=PACK, column=0, long=width):
        g = expert_sums[:, row : row + height, column : column + long].astype(F32)
        return g.reshape(n_exp, SETS, RANK, long).transpose(0, 3, 1, 2)

    low_rows = expert_sums[:, 4 * PACK :].astype(F32)
    low_rows = jnp.stack([low_rows[:, :, :ff], low_rows[:, :, ff:]], axis=1)
    expert_outs = [
        restore(0),
        restore(2 * PACK, long=ff),
        restore(PACK),
        restore(2 * PACK, column=ff, long=ff),
        low_rows.transpose(0, 3, 1, 2),
        restore(3 * PACK),
    ]
    return (output, input_grad, *attn_outs, *expert_outs)


def solution(mesh):
    rows = P(("rep", "shard"), None)
    second = P(None, "shard")
    three = P("shard", None, None)
    four = P("shard", None, None, None)
    placed = (rows,) * 6 + (P(("rep", "shard")), P(), P()) + (second,) * 4
    placed = placed + (three,) * 11 + (four,) * 6
    return jax.shard_map(
        functools.partial(local, mesh.shape["rep"], mesh.shape["shard"]),
        mesh=mesh,
        in_specs=placed,
        out_specs=(rows, rows) + (three,) * 8 + (four,) * 6,
        check_vma=False,
    )
```

```python
import functools

import jax
import jax.numpy as jnp
from jax import lax
from jax.experimental import pallas as pl
from jax.experimental.pallas import tpu as pltpu
from jax.sharding import PartitionSpec as P

HEADS = 16
HEAD = 128
TOP = 8
EXPERTS = 16
RANK = 16
SETS = 2
MOST = 160
PACK = SETS * RANK

epsilon = 1e-06
adapter_scale = 2.0
masked_score = -1e30
score_scale = HEAD ** (-0.5)

BF = jnp.bfloat16
F32 = jnp.float32
VMEM = 56 * 1024 * 1024


def dot_nn(a, b):
    return jnp.dot(a, b, preferred_element_type=F32)


def dot_nt(a, b):
    return lax.dot_general(a, b, (((1,), (1,)), ((), ())), preferred_element_type=F32)


def dot_tn(a, b):
    return lax.dot_general(a, b, (((0,), (0,)), ((), ())), preferred_element_type=F32)


def rms_forward(values, gain_vec):
    inverse = lax.rsqrt(jnp.mean(values * values, axis=-1, keepdims=True) + epsilon)
    return values * inverse * gain_vec


def rms_backward(values, gain_vec, grad_norm):
    inverse = lax.rsqrt(jnp.mean(values * values, axis=-1, keepdims=True) + epsilon)
    weighted = grad_norm * gain_vec
    cubed = inverse * inverse * inverse
    return inverse * weighted - values * cubed * jnp.mean(values * weighted, axis=-1, keepdims=True)


def scores(q, k, allowed):
    s = dot_nt(q, k) * score_scale
    s = jnp.where(allowed, s, masked_score)
    e = jnp.exp(s - jnp.max(s, axis=-1, keepdims=True))
    return e * (1.0 / jnp.sum(e, axis=-1, keepdims=True))


def allowed_mask(seg_row, seg_col, pad_row):
    shape = (seg_col.shape[0], seg_row.shape[1])
    rows = lax.broadcasted_iota(jnp.int32, shape, 0)
    cols = lax.broadcasted_iota(jnp.int32, shape, 1)
    return (seg_col == seg_row) & ((pad_row == 1) | (rows == cols))


def project_kernel(sizes, ids, h, downs, *refs):
    team, n_line, rows, width = sizes
    near, far, refs = refs[0], refs[1], refs[2:]
    outs, (r_own, h_s, flag_s, w_s, r_s, lift_s, sems) = refs[:team], refs[team:]
    plane, chip, core = ids[0], ids[1], ids[2]
    half = width // 2
    lift_half = 3 * PACK // 2
    copies = []
    for j in range(team):
        source = ids[3] + (chip ^ j) * 2 + core
        copies.append(
            pltpu.make_async_copy(
                h.at[source, :rows], h_s.at[j * rows : (j + 1) * rows], sems.at[0, j]
            )
        )
        copies.append(
            pltpu.make_async_copy(h.at[source, rows:, :HEAD], flag_s.at[j], sems.at[1, j])
        )
    for copy in copies:
        copy.start()
    for k in range(n_line):
        at = pl.ds(pl.multiple_of((plane + k) % n_line * HEAD, HEAD), HEAD)
        for side, ref in ((core, near), (1 - core, far)):
            for a in range(3):
                start = a * half + (lift_half if a else 0)
                w_s[a, pl.ds(pl.multiple_of(side * half, half), half), at] = ref[
                    k, start : start + half, :
                ]
            lift_s[3, pl.ds(pl.multiple_of(side * lift_half, 16), lift_half), at] = ref[
                k, half : half + lift_half, :
            ]
    lifts = lift_s[3]
    band = lax.broadcasted_iota(jnp.int32, lifts.shape, 0) // PACK
    for a in range(3):
        lift_s[a] = jnp.where(band == a, lifts, jnp.zeros_like(lifts))
    for copy in copies:
        copy.wait()
    for j in range(team):
        at = slice(j * rows, (j + 1) * rows)
        keep = flag_s[j, :1, : 3 * PACK].astype(F32)
        r_s[at, :] = (dot_nt(h_s[at, :], downs[: 3 * PACK, :]) * keep).astype(BF)
    for a in range(3):
        r_own[a] = r_s[:rows, a * PACK : (a + 1) * PACK]
    span = n_line * HEAD
    tile = min(256, span)
    per = span // tile

    def step(i, carry):
        a = i // per
        at = pl.multiple_of((i % per) * tile, tile)
        y = dot_nn(h_s[...], w_s[a, :, pl.ds(at, tile)])
        y = y + adapter_scale * dot_nn(r_s[...], lift_s[a, :, pl.ds(at, tile)])
        y = y.astype(BF)
        for j in range(team):
            outs[j][:, pl.ds(pl.multiple_of(i * tile, tile), tile)] = y[j * rows : (j + 1) * rows]
        return carry

    lax.fori_loop(0, 3 * per, step, 0)


def project(ids, h, downs, near, far, sizes):
    team, n_line, rows, width = sizes
    span = n_line * HEAD
    full = pl.BlockSpec(memory_space=pltpu.VMEM)
    got = pl.pallas_call(
        functools.partial(project_kernel, sizes),
        in_specs=[pl.BlockSpec(memory_space=pltpu.SMEM), pl.BlockSpec(memory_space=pl.ANY)]
        + [full] * 3,
        out_specs=[full] * (team + 1),
        out_shape=[jax.ShapeDtypeStruct((rows, 3 * span), BF)] * team
        + [jax.ShapeDtypeStruct((3, rows, PACK), BF)],
        scratch_shapes=[
            pltpu.VMEM((team * rows, width), BF),
            pltpu.VMEM((team, 16, HEAD), BF),
            pltpu.VMEM((3, width, span), BF),
            pltpu.VMEM((team * rows, 3 * PACK), BF),
            pltpu.VMEM((4, 3 * PACK, span), BF),
            pltpu.SemaphoreType.DMA((2, team)),
        ],
        compiler_params=pltpu.CompilerParams(vmem_limit_bytes=VMEM),
        cost_estimate=pl.CostEstimate(
            flops=6 * team * rows * width * span, bytes_accessed=12 * width * span, transcendentals=0
        ),
    )(ids, h, downs, near, far)
    return got[:team], got[team]


def chip_columns(ref, chip, n_line, cols):
    parts = []
    for z in range(n_line):
        parts.append(ref[:, pl.ds(pl.multiple_of(z * cols + chip * HEAD, HEAD), HEAD)])
    return jnp.concatenate(parts, axis=1)


def mix_kernel(sizes, ids, seg_row, seg_col, pad_row, tokens, gain, d_out, l_out, keep, *refs):
    team, n_line, rows, width, cols = sizes
    qkv, refs = refs[:team], refs[team:]
    near, refs = refs[:team], refs[team:]
    far, refs = refs[:team], refs[team:]
    mixed, r_out, x1, h2, acc = refs
    chip, core = ids[1], ids[2]
    span = n_line * HEAD
    side = span // 2
    allowed = allowed_mask(seg_row[...], seg_col[...], pad_row[...])
    reduced = jnp.zeros((rows, PACK), F32)
    for j in range(team):
        for z in range(n_line):
            q, k, v = (
                qkv[j][:, a * span + z * HEAD : a * span + (z + 1) * HEAD] for a in range(3)
            )
            p = scores(q, k, allowed)
            mixed[:, j * span + z * HEAD : j * span + (z + 1) * HEAD] = dot_nn(
                p.astype(BF), v
            ).astype(BF)
        o = mixed[:, j * span : (j + 1) * span]
        reduced = reduced + dot_nt(o, chip_columns(d_out, chip ^ j, n_line, cols))
        mine = mixed[:, pl.ds(pl.multiple_of(j * span + core * side, HEAD), side)]
        other = mixed[:, pl.ds(pl.multiple_of(j * span + (1 - core) * side, HEAD), side)]
        part = dot_nn(mine, near[j][...]) + dot_nn(other, far[j][...])
        if j == 0:
            acc[...] = part
        else:
            acc[...] += part
    low = (reduced * keep[...]).astype(BF)
    r_out[...] = low
    total = tokens[...].astype(F32) + (acc[...] + adapter_scale * dot_nn(low, l_out[...]))
    x1[...] = total
    h2[...] = rms_forward(total, gain[...]).astype(BF)


def mix(ids, masks, tokens, gain, d_out, l_out, keep, qkv, near, far, sizes):
    team, n_line, rows, width, cols = sizes
    full = pl.BlockSpec(memory_space=pltpu.VMEM)
    return pl.pallas_call(
        functools.partial(mix_kernel, sizes),
        in_specs=[pl.BlockSpec(memory_space=pltpu.SMEM)] + [full] * (8 + 3 * team),
        out_specs=[full] * 4,
        out_shape=[
            jax.ShapeDtypeStruct((rows, width), BF),
            jax.ShapeDtypeStruct((rows, PACK), BF),
            jax.ShapeDtypeStruct((rows, width), F32),
            jax.ShapeDtypeStruct((rows, width), BF),
        ],
        scratch_shapes=[pltpu.VMEM((rows, width), F32)],
        compiler_params=pltpu.CompilerParams(vmem_limit_bytes=VMEM),
        cost_estimate=pl.CostEstimate(
            flops=2 * rows * width * width + 4 * rows * rows * width,
            bytes_accessed=2 * width * width + 12 * rows * width,
            transcendentals=rows * rows * HEADS,
        ),
    )(ids, *masks, tokens, gain, d_out, l_out, keep, *qkv, *near, *far)


def back_kernel(sizes, n_parts, ids, *refs):
    team, n_line, rows, width, cols = sizes
    (seg_row, seg_col, pad_row, tokens, cot, x1, gain1, gain2, own, downs, l_out, keep) = refs[:12]
    refs = refs[12:]
    parts, refs = refs[:n_parts], refs[n_parts:]
    mixed, r_own, r_out = refs[:3]
    refs = refs[3:]
    qkv, refs = refs[:team], refs[team:]
    near_o, refs = refs[:team], refs[team:]
    far_o, refs = refs[:team], refs[team:]
    weights, in_grad, grads, near_s, far_s, sems, dx1_s, da_s, do_s, do_b, dp_s, acc, h1_s, dr, lift_s = refs
    chip, core = ids[1], ids[2]
    span = n_line * HEAD
    side = span // 2
    half = width // 2
    lift_gap = 3 * PACK // 2
    lift_end = half + lift_gap
    slots = near_s.shape[0]

    def fetch(j):
        copies = []
        for side_at, buf in ((core, near_s), (1 - core, far_s)):
            source = ids[3] + (chip ^ j) * 2 + side_at
            number = 0 if buf is near_s else 1
            for z in range(n_line):
                at = pl.multiple_of((ids[0] + z) % n_line * HEAD, HEAD)
                copies.append(
                    pltpu.make_async_copy(
                        weights.at[source, z],
                        buf.at[j % slots, :, pl.ds(at, HEAD)],
                        sems.at[j % slots, number, z],
                    )
                )
        return copies

    for copy in fetch(0):
        copy.start()
    mask = keep[...]
    dh2 = own[...]
    for part in parts:
        dh2 = dh2 + part[...].astype(F32)
    dx1 = cot[...].astype(F32) + rms_backward(x1[...], gain2[...], dh2)
    dx1_s[...] = dx1
    da_s[...] = dx1.astype(BF)
    h1_s[...] = rms_forward(tokens[...].astype(F32), gain1[...]).astype(BF)
    da = da_s[...]
    d_low = (adapter_scale * dot_nt(da, l_out[...]) * mask).astype(BF)

    def put_all(row, block):
        for z in range(n_line):
            part = block[:, z * cols : (z + 1) * cols]
            grads[z, row : row + RANK, :] = (part[:RANK] + part[RANK:]).astype(BF)

    put_all(7 * RANK, adapter_scale * dot_tn(r_out[...], da))
    allowed = allowed_mask(seg_row[...], seg_col[...], pad_row[...])
    dr[...] = jnp.zeros_like(dr)
    here = pl.multiple_of(core * half, half)
    there = pl.multiple_of((1 - core) * half, half)
    acc[...] = jnp.zeros_like(acc)
    for j in range(team):
        ahead = j + slots - 1
        if 0 < ahead < team:
            for copy in fetch(ahead):
                copy.start()
        spot = chip ^ j

        def put(row, block):
            for z in range(n_line):
                at = pl.multiple_of(spot * HEAD, HEAD)
                part = block[:, z * HEAD : (z + 1) * HEAD]
                part = part[:RANK] + part[RANK:]
                grads[z, pl.ds(row, RANK), pl.ds(at, HEAD)] = part.astype(BF)

        do_s[:, pl.ds(pl.multiple_of(core * side, HEAD), side)] = dot_nt(da, near_o[j][...])
        do_s[:, pl.ds(pl.multiple_of((1 - core) * side, HEAD), side)] = dot_nt(da, far_o[j][...])
        do = do_s[...] + dot_nn(
            d_low, chip_columns(downs.at[3 * PACK :, :], spot, n_line, cols)
        )
        do = do.astype(BF)
        put(3 * RANK, dot_tn(d_low, mixed[:, j * span : (j + 1) * span]))
        do_b[...] = do

        def head(z, carry):
            at = pl.multiple_of(z * HEAD, HEAD)
            q, k, v = (
                qkv[j][:, pl.ds(pl.multiple_of(a * span + at, HEAD), HEAD)] for a in range(3)
            )
            p = scores(q, k, allowed)
            do_h = do_b[:, pl.ds(at, HEAD)]
            dp = dot_nt(do_h, v)
            delta = jnp.sum(dp * p, axis=-1, keepdims=True)
            ds = (p * (dp - delta)).astype(BF)
            heads = (
                dot_nn(ds, k) * score_scale,
                dot_tn(ds, q) * score_scale,
                dot_tn(p.astype(BF), do_h),
            )
            for a in range(3):
                dp_s[:, pl.ds(pl.multiple_of(a * span + at, HEAD), HEAD)] = heads[a].astype(BF)
            return carry

        lax.fori_loop(0, n_line, head, 0, unroll=2)
        for copy in fetch(j):
            copy.wait()
        slot = j % slots
        packs = jnp.where(
            core == 0,
            jnp.concatenate([near_s[slot, half:lift_end, :], far_s[slot, half:lift_end, :]]),
            jnp.concatenate([far_s[slot, half:lift_end, :], near_s[slot, half:lift_end, :]]),
        )
        for a in range(3):
            lift_s[a] = packs[a * PACK : (a + 1) * PACK]

        near_sum, far_sum = None, None
        for a in range(3):
            g = dp_s[:, a * span : (a + 1) * span]
            dr[a] += dot_nt(g, lift_s[a])
            put((4 + a) * RANK, adapter_scale * dot_tn(r_own[a], g))
            start = a * half + (lift_gap if a else 0)
            near_part = dot_nt(g, near_s[slot, start : start + half, :])
            far_part = dot_nt(g, far_s[slot, start : start + half, :])
            near_sum = near_part if a == 0 else near_sum + near_part
            far_sum = far_part if a == 0 else far_sum + far_part
        acc[:, pl.ds(here, half)] += near_sum
        acc[:, pl.ds(there, half)] += far_sum
    h1 = h1_s[...]
    for a in range(3):
        low = (adapter_scale * dr[a] * mask).astype(BF)
        put_all(a * RANK, dot_tn(low, h1))
        acc[...] += dot_nn(low, downs[a * PACK : (a + 1) * PACK, :])
    total = dx1_s[...] + rms_backward(tokens[...].astype(F32), gain1[...], acc[...])
    in_grad[...] = total.astype(BF)


def attention_back(ids, small, parts, kept, qkv, near_o, far_o, weights, sizes):
    team, n_line, rows, width, cols = sizes
    span = n_line * HEAD
    full = pl.BlockSpec(memory_space=pltpu.VMEM)
    count = len(small) + len(parts) + len(kept) + 3 * team
    slots = 2 if span <= 512 else 1
    return pl.pallas_call(
        functools.partial(back_kernel, sizes, len(parts)),
        in_specs=[pl.BlockSpec(memory_space=pltpu.SMEM)]
        + [full] * count
        + [pl.BlockSpec(memory_space=pl.ANY)],
        out_specs=[full] * 2,
        out_shape=[
            jax.ShapeDtypeStruct((rows, width), BF),
            jax.ShapeDtypeStruct((n_line, 8 * RANK, cols), BF),
        ],
        scratch_shapes=[
            pltpu.VMEM((slots, weights.shape[2], span), BF),
            pltpu.VMEM((slots, weights.shape[2], span), BF),
            pltpu.SemaphoreType.DMA((slots, 2, n_line)),
            pltpu.VMEM((rows, width), F32),
            pltpu.VMEM((rows, width), BF),
            pltpu.VMEM((rows, span), F32),
            pltpu.VMEM((rows, span), BF),
            pltpu.VMEM((rows, 3 * span), BF),
            pltpu.VMEM((rows, width), F32),
            pltpu.VMEM((rows, width), BF),
            pltpu.VMEM((3, rows, PACK), F32),
            pltpu.VMEM((3, PACK, span), BF),
        ],
        compiler_params=pltpu.CompilerParams(vmem_limit_bytes=VMEM),
        cost_estimate=pl.CostEstimate(
            flops=8 * rows * width * width + 10 * rows * rows * width,
            bytes_accessed=8 * width * width + 20 * rows * width,
            transcendentals=rows * rows * HEADS,
        ),
    )(ids, *small, *parts, *kept, *qkv, *near_o, *far_o, weights)


def expert_kernel(
    n_exp,
    has_sum,
    tile,
    source,
    h2,
    place,
    weight,
    mask,
    dy_in,
    dm_in,
    drl_in,
    w_gate,
    w_up,
    w_low,
    d_gu,
    l_gate,
    l_up,
    d_low,
    l_low,
    *refs,
):
    prior = None
    if has_sum:
        prior, refs = refs[0], refs[1:]
    (out, dh2, grads) = refs[:3]
    (x_s, hid_s, dg_s, du_s, sel, y_all, dx_all, gate_s, up_s, low_s, sems) = refs[3:]
    ff = w_gate.shape[2]

    def emit(row, value, column=0):
        at = (0, slice(row, row + value.shape[0]), slice(column, column + value.shape[1]))
        if has_sum:
            value = value + prior[at]
        grads[at] = value.astype(grads.dtype)

    e = pl.program_id(0)
    slot = e % 2

    def fetch(number):
        pairs = ((w_gate, gate_s), (w_up, up_s), (w_low, low_s))
        return [
            pltpu.make_async_copy(w.at[number], buf.at[number % 2], sems.at[number % 2, i])
            for i, (w, buf) in enumerate(pairs)
        ]

    @pl.when(e == 0)
    def _():
        for copy in fetch(e):
            copy.start()

    @pl.when(e + 1 < n_exp)
    def _():
        for copy in fetch(e + 1):
            copy.start()

    ready = fetch(e)
    keep = mask[...]
    keep_one = keep[:, :PACK]
    base = pl.multiple_of(e * MOST, MOST)
    slots = lax.broadcasted_iota(jnp.int32, (MOST, place.shape[2]), 0)
    hit = slots == place[0]
    pick = jnp.where(hit, 1.0, 0.0).astype(BF)
    sel[pl.ds(base, MOST), :] = pick
    sw = jnp.sum(jnp.where(hit, weight[0], 0.0), axis=1, keepdims=True)
    x_s[...] = dot_nn(pick, h2[...]).astype(BF)
    x = x_s[...]
    dy = dy_in[0, 0]
    r_gu = (dot_nt(x, d_gu[0]) * keep).astype(BF)
    r_g, r_u = r_gu[:, :PACK], r_gu[:, PACK:]
    dr_low = drl_in[0, 0]
    ready[0].wait()
    ready[1].wait()
    for start in range(0, w_gate.shape[2], tile):
        at = slice(start, start + tile)
        gate = dot_nn(x, gate_s[slot, :, at]) + adapter_scale * dot_nn(r_g, l_gate[0, :, at])
        up = dot_nn(x, up_s[slot, :, at]) + adapter_scale * dot_nn(r_u, l_up[0, :, at])
        d_hidden = dm_in[0, 0, :, at].astype(F32)
        sig = 1.0 / (1.0 + jnp.exp(-gate))
        act = gate * sig
        hid_s[:, at] = (act * up).astype(BF)
        dg_s[:, at] = (d_hidden * up * sig * (1.0 + gate * (1.0 - sig))).astype(BF)
        du_s[:, at] = (d_hidden * act).astype(BF)
    hidden, d_gate, d_up = hid_s[...], dg_s[...], du_s[...]
    r_low = (dot_nt(hidden, d_low[0]) * keep_one).astype(BF)
    ready[2].wait()
    y = dot_nn(hidden, low_s[slot]) + adapter_scale * dot_nn(r_low, l_low[0])
    y_all[pl.ds(base, MOST), :] = (y * sw).astype(BF)
    dr = jnp.concatenate([dot_nt(d_gate, l_gate[0]), dot_nt(d_up, l_up[0])], axis=1)
    dr = (adapter_scale * dr * keep).astype(BF)
    dx = dot_nt(d_gate, gate_s[slot]) + dot_nt(d_up, up_s[slot]) + dot_nn(dr, d_gu[0])
    dx_all[pl.ds(base, MOST), :] = dx.astype(BF)
    emit(0, dot_tn(dr, x))
    emit(2 * PACK, adapter_scale * dot_tn(r_g, d_gate))
    emit(2 * PACK, adapter_scale * dot_tn(r_u, d_up), ff)
    emit(3 * PACK, adapter_scale * dot_tn(r_low, dy))
    g_low = dot_tn(dr_low, hidden)
    emit(4 * PACK, g_low[:RANK])
    emit(4 * PACK, g_low[RANK:], ff)

    @pl.when(e == n_exp - 1)
    def _():
        out[...] = dot_tn(sel[...], y_all[...]).astype(out.dtype)
        dh2[...] = dot_tn(sel[...], dx_all[...]).astype(dh2.dtype)


def grad_kernel(n_line, tile, cot, place, weight, mask, w_low, d_low, l_low, dy, dm, drl, dy_s):
    slots = lax.broadcasted_iota(jnp.int32, (MOST, place.shape[3]), 0)
    for k in range(n_line):
        hit = slots == place[k, 0]
        pick = jnp.where(hit, 1.0, 0.0).astype(BF)
        sw = jnp.sum(jnp.where(hit, weight[k, 0], 0.0), axis=1, keepdims=True)
        block = (dot_nn(pick, cot[k]) * sw).astype(BF)
        dy_s[k * MOST : (k + 1) * MOST, :] = block
        dy[k, 0] = block
    full = dy_s[...]
    dr = adapter_scale * dot_nt(full, l_low[0])
    dr = jnp.concatenate(
        [dr[k * MOST : (k + 1) * MOST] * mask[k, :, :PACK] for k in range(n_line)], axis=0
    ).astype(BF)
    for k in range(n_line):
        drl[k, 0] = dr[k * MOST : (k + 1) * MOST]
    for start in range(0, w_low.shape[1], tile):
        at = slice(start, start + tile)
        block = dot_nt(full, w_low[0, at, :]) + dot_nn(dr, d_low[0, :, at])
        block = block.astype(BF)
        for k in range(n_line):
            dm[k, 0, :, at] = block[k * MOST : (k + 1) * MOST]


def grad_rows(cot, place, weight, mask, w_low, d_low, l_low):
    n_line, rows, width = cot.shape
    n_exp, ff = w_low.shape[:2]
    per_e = lambda e: (e, 0, 0)
    all_e = lambda e: (0, e, 0, 0)
    return pl.pallas_call(
        functools.partial(grad_kernel, n_line, 256),
        grid=(n_exp,),
        in_specs=[
            pl.BlockSpec((n_line, rows, width), lambda e: (0, 0, 0)),
            pl.BlockSpec((n_line, 1, 1, rows), all_e),
            pl.BlockSpec((n_line, 1, 1, rows), all_e),
            pl.BlockSpec((n_line, 1, 2 * PACK), lambda e: (0, 0, 0)),
            pl.BlockSpec((1, ff, width), per_e),
            pl.BlockSpec((1, PACK, ff), per_e),
            pl.BlockSpec((1, PACK, width), per_e),
        ],
        out_specs=[
            pl.BlockSpec((n_line, 1, MOST, width), all_e),
            pl.BlockSpec((n_line, 1, MOST, ff), all_e),
            pl.BlockSpec((n_line, 1, MOST, PACK), all_e),
        ],
        out_shape=[
            jax.ShapeDtypeStruct((n_line, n_exp, MOST, width), BF),
            jax.ShapeDtypeStruct((n_line, n_exp, MOST, ff), BF),
            jax.ShapeDtypeStruct((n_line, n_exp, MOST, PACK), BF),
        ],
        scratch_shapes=[pltpu.VMEM((n_line * MOST, width), BF)],
        compiler_params=pltpu.CompilerParams(
            vmem_limit_bytes=VMEM, dimension_semantics=("arbitrary",)
        ),
        cost_estimate=pl.CostEstimate(
            flops=3 * n_line * n_exp * MOST * width * ff,
            bytes_accessed=2 * n_exp * width * ff,
            transcendentals=0,
        ),
    )(cot, place, weight, mask, w_low, d_low, l_low)


def expert_chunk(source, h2, ready, place, weight, mask, params, prior, out_type, grad_type=F32):
    w_gate, w_up, w_low, d_gu, l_gate, l_up, d_low, l_low = params
    n_exp, width, ff = w_gate.shape
    rows = h2.shape[0]
    whole = lambda e, s: (0, 0)
    per_e = lambda e, s: (e, 0, 0)
    grad_specs = [pl.BlockSpec((1, 4 * PACK + RANK, width), per_e)]
    return pl.pallas_call(
        functools.partial(expert_kernel, n_exp, prior is not None, 256),
        grid_spec=pltpu.PrefetchScalarGridSpec(
            num_scalar_prefetch=1,
            grid=(n_exp,),
            in_specs=[
                pl.BlockSpec((rows, width), whole),
                pl.BlockSpec((1, 1, rows), per_e),
                pl.BlockSpec((1, 1, rows), per_e),
                pl.BlockSpec((1, 2 * PACK), whole),
                pl.BlockSpec((1, 1, MOST, width), lambda e, s: (s[0], e, 0, 0)),
                pl.BlockSpec((1, 1, MOST, ff), lambda e, s: (s[0], e, 0, 0)),
                pl.BlockSpec((1, 1, MOST, PACK), lambda e, s: (s[0], e, 0, 0)),
                pl.BlockSpec(memory_space=pl.ANY),
                pl.BlockSpec(memory_space=pl.ANY),
                pl.BlockSpec(memory_space=pl.ANY),
                pl.BlockSpec((1, 2 * PACK, width), per_e),
                pl.BlockSpec((1, PACK, ff), per_e),
                pl.BlockSpec((1, PACK, ff), per_e),
                pl.BlockSpec((1, PACK, ff), per_e),
                pl.BlockSpec((1, PACK, width), per_e),
            ]
            + (grad_specs if prior is not None else []),
            out_specs=[
                pl.BlockSpec((rows, width), whole),
                pl.BlockSpec((rows, width), whole),
            ]
            + grad_specs,
            scratch_shapes=[
                pltpu.VMEM((MOST, width), BF),
                pltpu.VMEM((MOST, ff), BF),
                pltpu.VMEM((MOST, ff), BF),
                pltpu.VMEM((MOST, ff), BF),
                pltpu.VMEM((n_exp * MOST, rows), BF),
                pltpu.VMEM((n_exp * MOST, width), BF),
                pltpu.VMEM((n_exp * MOST, width), BF),
                pltpu.VMEM((2, width, ff), BF),
                pltpu.VMEM((2, width, ff), BF),
                pltpu.VMEM((2, ff, width), BF),
                pltpu.SemaphoreType.DMA((2, 3)),
            ],
        ),
        out_shape=[
            jax.ShapeDtypeStruct((rows, width), out_type),
            jax.ShapeDtypeStruct((rows, width), out_type),
        ]
        + [jax.ShapeDtypeStruct((n_exp, 4 * PACK + RANK, width), grad_type)],
        compiler_params=pltpu.CompilerParams(
            vmem_limit_bytes=VMEM, dimension_semantics=("arbitrary",)
        ),
        cost_estimate=pl.CostEstimate(
            flops=16 * n_exp * MOST * width * ff,
            bytes_accessed=6 * n_exp * width * ff,
            transcendentals=n_exp * MOST * ff,
        ),
    )(
        source,
        h2,
        place,
        weight,
        mask,
        *ready,
        w_gate,
        w_up,
        w_low,
        d_gu,
        l_gate,
        l_up,
        d_low,
        l_low,
        *(prior or ()),
    )


def local(
    n_rep,
    n_shard,
    tokens,
    cotangent,
    segments,
    padding,
    routes,
    route_weights,
    adapter_set,
    norm_one,
    norm_two,
    query_weight,
    key_weight,
    value_weight,
    output_weight,
    query_down,
    key_down,
    value_down,
    output_down,
    query_lift,
    key_lift,
    value_lift,
    output_lift,
    expert_gate,
    expert_upper,
    expert_lower,
    gate_down,
    gate_lift,
    upper_down,
    upper_lift,
    lower_down,
    lower_lift,
):
    seq_len, width = tokens.shape
    n_exp, _, ff = expert_gate.shape
    cols = query_weight.shape[1]
    team = min(cols // HEAD, n_rep // 2)
    tiles = cols // HEAD
    half = width // 2
    plane = lax.axis_index("shard")
    rep = lax.axis_index("rep")
    core = rep % 2
    chip = (rep // 2) % team
    ids = jnp.stack([plane, chip, core, rep - rep % (2 * team)]).astype(jnp.int32)

    def rep_swap(x, bits):
        return lax.ppermute(x, "rep", [(a, a ^ bits) for a in range(n_rep)])

    def line_step(up, down):
        return (
            lax.ppermute(up, "shard", [(a, a - 1) for a in range(1, n_shard)]),
            lax.ppermute(down, "shard", [(a, a + 1) for a in range(n_shard - 1)]),
        )

    def line_steps(x):
        steps = [(x, x)]
        for _ in range(1, n_shard):
            steps.append(line_step(*steps[-1]))
        return steps

    def line_join(steps):
        joined = [steps[0][0]]
        for k in range(1, n_shard):
            joined.append(steps[k][0] + steps[n_shard - k][1])
        return joined

    def line_send(x, k):
        return lax.ppermute(x, "shard", [(a, (a + k) % n_shard) for a in range(n_shard)])

    def in_order(parts):
        buf = jnp.zeros((n_shard,) + parts[0].shape, parts[0].dtype)
        for k, part in enumerate(parts):
            buf = lax.dynamic_update_index_in_dim(buf, part, (plane + k) % n_shard, 0)
        return buf

    def chip_gather(x):
        return [x] + [rep_swap(x, j << 1) for j in range(1, team)]

    def after(x, *others):
        return lax.optimization_barrier((x,) + others)[0]

    chosen_set = adapter_set[0]
    set_flags = (jnp.arange(SETS, dtype=jnp.int32) == chosen_set).astype(F32)
    keep = jnp.repeat(set_flags, RANK)[None]
    masks = (segments, segments.reshape(seq_len, 1), padding)
    gain_one, gain_two = norm_one[None], norm_two[None]
    normed_one = rms_forward(tokens.astype(F32), gain_one).astype(BF)
    flag_rows = jnp.pad(jnp.tile(keep, (16, 3)), ((0, 0), (0, width - 3 * PACK))).astype(BF)
    all_h = lax.all_gather(jnp.concatenate([normed_one, flag_rows], axis=0), "rep")

    expert_ids = jnp.arange(EXPERTS, dtype=jnp.int32)
    picked = routes[:, :, None] == expert_ids[None, None, :]
    member = jnp.sum(picked.astype(jnp.int32), axis=1)
    before = jnp.cumsum(member, axis=0) - member
    place = jnp.where(member == 1, before, -1).T.astype(F32)
    per_expert = jnp.sum(jnp.where(picked, route_weights[:, :, None], 0.0), axis=1).T
    high = lax.reduce_precision(per_expert, 8, 7)
    mid = lax.reduce_precision(per_expert - high, 8, 7)
    low = per_expert - high - mid
    flag = jnp.broadcast_to(chosen_set.astype(F32), (EXPERTS, seq_len))
    info = jnp.concatenate([place, high, mid, low, flag], axis=0).astype(BF)
    fact_rows = info.size // HEAD

    def flat(table):
        return table.reshape(table.shape[0], PACK).T

    def pieces(x):
        return x.reshape(x.shape[0], tiles, HEAD).transpose(1, 0, 2).reshape(-1, HEAD)

    def whole_rows(x, height):
        x = x.reshape(n_shard, tiles, height, HEAD)
        return x.transpose(2, 0, 1, 3).reshape(height, width)

    def both(a, b, axis=0):
        return jnp.where(
            core == 0, jnp.concatenate([a, b], axis=axis), jnp.concatenate([b, a], axis=axis)
        )

    def slice_of(weight):
        return lax.dynamic_slice(weight, (core * half, chip * HEAD), (half, HEAD))

    def core_rows(table, height):
        return lax.dynamic_slice(table, (core * height, 0), (height, table.shape[1]))

    lift_rows = 3 * PACK // 2
    down_rows = 4 * PACK // 2
    last_rows = PACK // 2
    lift_pack = jnp.concatenate([flat(t) for t in (query_lift, key_lift, value_lift)], axis=0)
    down_pack = jnp.concatenate(
        [flat(t) for t in (query_down, key_down, value_down, output_down)], axis=0
    )
    out_rows = output_weight.reshape(2, n_shard // 2, tiles, HEAD, cols)
    out_own = lax.dynamic_slice(
        out_rows, (core, 0, chip, 0, 0), (1, n_shard // 2, 1, HEAD, cols)
    ).reshape(n_shard // 2 * HEAD, cols)
    first = [
        pieces(core_rows(down_pack, down_rows)),
        pieces(core_rows(flat(output_lift), last_rows)),
        info.reshape(fact_rows, HEAD),
        pieces(out_own),
    ]
    marks = [0]
    for piece in first:
        marks.append(marks[-1] + piece.shape[0])
    second = [
        slice_of(query_weight),
        lax.dynamic_slice(lift_pack, (core * lift_rows, chip * HEAD), (lift_rows, HEAD)),
        slice_of(key_weight),
        slice_of(value_weight),
    ]
    steps1 = line_steps(jnp.concatenate(first, axis=0))
    line1 = line_join(steps1)
    near1 = in_order(line1)
    out_block = whole_rows(near1[:, marks[3] :], n_shard // 2 * HEAD)
    steps2 = [(after(jnp.concatenate(second, axis=0), *steps1[-2]),) * 2]
    for number in range(1, n_shard):
        last = steps2[-1]
        steps2.append(line_step(*(after(last, out_block) if number == 2 else last)))
    line2 = jnp.stack(line_join(steps2))
    far1 = rep_swap(near1[:, : marks[2]], 1)
    downs = both(*(whole_rows(g[:, : marks[1]], down_rows) for g in (near1, far1)))
    lift_out = both(*(whole_rows(g[:, marks[1] : marks[2]], last_rows) for g in (near1, far1)))
    near_o = chip_gather(out_block)
    far2 = rep_swap(line2, 1)

    params = (
        expert_gate,
        expert_upper,
        expert_lower,
        jnp.concatenate(
            [t.reshape(n_exp, width, PACK).transpose(0, 2, 1) for t in (gate_down, upper_down)],
            axis=1,
        ),
        gate_lift.reshape(n_exp, -1, PACK).transpose(0, 2, 1),
        upper_lift.reshape(n_exp, -1, PACK).transpose(0, 2, 1),
        lower_down.reshape(n_exp, -1, PACK).transpose(0, 2, 1),
        lower_lift.reshape(n_exp, width, PACK).transpose(0, 2, 1),
    )

    def read(facts):
        mine = lax.dynamic_slice_in_dim(facts.astype(F32), plane * n_exp, n_exp, 2)
        flags = (jnp.arange(SETS, dtype=F32) == mine[:, 4, 0, :1]).astype(F32)
        mask = jnp.tile(jnp.repeat(flags, RANK, axis=1), (1, 2))
        return mine[:, 0].astype(jnp.int32), mine[:, 1] + mine[:, 2] + mine[:, 3], mask

    line_facts = read(near1[:, marks[2] : marks[3]].reshape(n_shard, 5, EXPERTS, seq_len))

    sizes = (team, n_shard, seq_len, width)
    made, r_own = project(ids, all_h, downs, line2, far2, sizes)
    near_o = after(tuple(near_o), *made)
    far_o = [rep_swap(b, 1) for b in near_o]
    qkv = [made[0]] + [rep_swap(made[j], j << 1) for j in range(1, team)]
    sizes = sizes + (cols,)
    mixed, r_out, after_attn, normed_two = mix(
        ids, masks, tokens, gain_two, downs[3 * PACK :], lift_out, keep, qkv, near_o, far_o, sizes
    )

    table = [
        sorted((b for b in range(n_shard) if b != a), key=lambda b, a=a: (abs(a - b), a - b))
        for a in range(n_shard)
    ]

    def slot_facts(number):
        source = plane.astype(jnp.int32)
        if number is not None:
            source = sum(jnp.where(plane == a, t[number], 0) for a, t in enumerate(table))
            source = source.astype(jnp.int32)
        spot, share_of, mask = (
            lax.dynamic_index_in_dim(f, source, 0, keepdims=False) for f in line_facts
        )
        return source.reshape(1), spot[:, None], share_of[:, None], mask[None]

    facts_of = {number: slot_facts(number) for number in (*range(n_shard - 1), None)}
    early = [f for facts in facts_of.values() for f in facts]
    cot_line = lax.all_gather(
        after(cotangent, line2, all_h, *params, *line_facts, *early), "shard"
    )
    all_w = lax.all_gather(after(line2, normed_two), "rep")
    row_steps = [(normed_two, normed_two)]
    row_steps.append(line_step(*row_steps[0]))

    def choose(options):
        groups = []
        for a, array in options.items():
            for group in groups:
                if group[0] is array:
                    group[1].append(a)
                    break
            else:
                groups.append((array, [a]))
        value = groups[0][0]
        for array, planes in groups[1:]:
            here = plane == planes[0]
            for a in planes[1:]:
                here = here | (plane == a)
            value = jnp.where(here, array, value)
        return value

    def slot_rows(number):
        options = {}
        for a in range(n_shard):
            far = table[a][number] - a
            options[a] = row_steps[far][0] if far > 0 else row_steps[-far][1]
        return choose(options)

    def send_back(x, number):
        rounds = []
        for a in range(n_shard):
            pair = (a, table[a][number])
            for pairs in rounds:
                if all(pair[1] != q[1] for q in pairs):
                    pairs.append(pair)
                    break
            else:
                rounds.append([pair])
        return [lax.ppermute(x, "shard", pairs) for pairs in rounds]

    spots, shares, set_masks = line_facts
    ready = grad_rows(
        cot_line,
        spots[:, :, None],
        shares[:, :, None],
        set_masks[:, None],
        after(expert_lower, normed_two),
        params[6],
        params[7],
    )

    row_steps[1] = after(row_steps[1], ready[1])
    row_steps.append(line_step(*row_steps[1]))

    def chunk(number, prior, waits):
        rows = normed_two if number is None else slot_rows(number)
        source, spot, share_of, mask = facts_of[number]
        if waits:
            rows = after(rows, *waits)
        return expert_chunk(
            source,
            rows,
            ready,
            spot,
            share_of,
            mask,
            params,
            prior,
            F32 if number is None else BF,
            BF if number is None else F32,
        )

    results, prior, parts = [], None, []
    for number in range(n_shard - 1):
        waits = parts[-2] if number > 1 else ()
        results.append(chunk(number, prior, waits))
        prior = results[-1][2:]
        parts.append(send_back(results[-1][1], number))
        done = number + 2
        if done < n_shard:
            row_steps[done] = after(row_steps[done], results[-1][1])
            if done + 1 < n_shard:
                row_steps.append(line_step(*row_steps[done]))
    own = chunk(None, prior, parts[-2] if n_shard > 2 else ())
    back_parts = [part for pair in parts for part in pair]
    prior, dh2 = own[2:], own[1]
    if len(back_parts) > 6:
        dh2 = dh2 + sum(part.astype(F32) for part in back_parts)
        back_parts = []

    def partial_for(far):
        options = {}
        for a in range(n_shard):
            if 0 <= a + far < n_shard:
                options[a] = results[table[a].index(a + far)][0]
        return choose(options).astype(F32)

    out_steps, up, down = [], None, None
    for far in range(n_shard - 1, 0, -1):
        right, left = partial_for(far), partial_for(-far)
        if up is not None:
            if far == n_shard - 2:
                up, down = after((up, down), own[1])
            right, left = right + up.astype(F32), left + down.astype(F32)
        up = lax.ppermute(
            right.astype(BF), "shard", [(a, a + 1) for a in range(n_shard - far)]
        )
        down = lax.ppermute(
            left.astype(BF), "shard", [(a, a - 1) for a in range(far, n_shard)]
        )
        out_steps.append((up, down))
    pack_shape = prior[0].shape
    split = prior[0].reshape(2, -1, width)
    taken = rep_swap(lax.dynamic_index_in_dim(split, 1 - core, 0, keepdims=False), 1)

    input_grad, attn_flat = attention_back(
        ids,
        (*masks, after(tokens, *out_steps[0]), cotangent, after_attn, gain_one, gain_two, dh2)
        + (downs, lift_out, keep),
        back_parts,
        (mixed, r_own, r_out),
        qkv,
        near_o,
        far_o,
        all_w,
        sizes,
    )
    taken = after(taken, attn_flat)
    mine = lax.dynamic_index_in_dim(split, core, 0, keepdims=False).astype(F32)
    split = (mine + taken.astype(F32)).astype(BF).reshape(team, -1, width)
    chip_total = lax.dynamic_index_in_dim(split, chip, 0, keepdims=False).astype(F32)
    expert_parts = [
        rep_swap(lax.dynamic_index_in_dim(split, chip ^ j, 0, keepdims=False), j << 1)
        for j in range(1, team)
    ]
    for part in expert_parts:
        chip_total = chip_total + part.astype(F32)
    for b in range(team.bit_length(), n_rep.bit_length() - 1):
        rounded = chip_total.astype(BF)
        chip_total = rounded.astype(F32) + rep_swap(rounded, 1 << b).astype(F32)
    rounded = chip_total.astype(BF)
    half_total = jnp.zeros((team,) + rounded.shape, BF)
    for j, part in enumerate(chip_gather(rounded)):
        half_total = lax.dynamic_update_index_in_dim(half_total, part, chip ^ j, 0)
    expert_sums = both(half_total[None], rep_swap(half_total, 1)[None]).reshape(pack_shape)
    if n_shard > 2:
        attn_flat = after(attn_flat, *out_steps[-2])
    output = after_attn + own[0] + up.astype(F32) + down.astype(F32)
    output = output.astype(BF)

    def block_of(k):
        return lax.dynamic_index_in_dim(attn_flat, (plane + k) % n_shard, 0, keepdims=False)

    def placed(part, k):
        own_set = lax.dynamic_index_in_dim(set_masks[:, RANK], (plane - k) % n_shard, 0)
        hit = own_set == jnp.arange(SETS, dtype=F32)
        return jnp.where(hit[:, None, None], part.astype(F32)[None], 0.0)

    total = placed(block_of(0), 0)
    for k in range(1, n_shard):
        total = total + placed(line_send(block_of(k), k), k)
    rounded = total.astype(BF)
    total = rounded.astype(F32) + rep_swap(rounded, 1).astype(F32)
    total = lax.dynamic_index_in_dim(total, core, 0, keepdims=False)
    bits = n_rep.bit_length() - 1
    stages = [[2, 4, 6]] if bits > 2 else [[1 << b] for b in range(1, bits)]
    stages = stages + [[1 << b] for b in range(3, bits)]
    for stage in stages:
        rounded = total.astype(BF)
        total = rounded.astype(F32)
        for swap in stage:
            total = total + rep_swap(rounded, swap).astype(F32)
    rounded = total.astype(BF)
    attn_flat = both(rounded[None], rep_swap(rounded, 1)[None]).astype(F32)

    def unflat(g):
        return g.transpose(2, 0, 1)

    attn_outs = [unflat(attn_flat[:, a * RANK : (a + 1) * RANK]) for a in range(8)]

    def restore(row, height=PACK, column=0, long=width):
        g = expert_sums[:, row : row + height, column : column + long].astype(F32)
        return g.reshape(n_exp, SETS, RANK, long).transpose(0, 3, 1, 2)

    low_rows = expert_sums[:, 4 * PACK :].astype(F32)
    low_rows = jnp.stack([low_rows[:, :, :ff], low_rows[:, :, ff:]], axis=1)
    expert_outs = [
        restore(0),
        restore(2 * PACK, long=ff),
        restore(PACK),
        restore(2 * PACK, column=ff, long=ff),
        low_rows.transpose(0, 3, 1, 2),
        restore(3 * PACK),
    ]
    return (output, input_grad, *attn_outs, *expert_outs)


def solution(mesh):
    rows = P(("rep", "shard"), None)
    second = P(None, "shard")
    three = P("shard", None, None)
    four = P("shard", None, None, None)
    placed = (rows,) * 6 + (P(("rep", "shard")), P(), P()) + (second,) * 4
    placed = placed + (three,) * 11 + (four,) * 6
    return jax.shard_map(
        functools.partial(local, mesh.shape["rep"], mesh.shape["shard"]),
        mesh=mesh,
        in_specs=placed,
        out_specs=(rows, rows) + (three,) * 8 + (four,) * 6,
        check_vma=False,
    )
```
